128 devices in a mesh: tm: 8 (over z, x_hi), space: 16 (over x_lo, y, core).
Axes of the slice: x: 4 (x_hi: 2, x_lo: 2; x = x_hi * 2 + x_lo), y: 4, z: 4, core: 2. Of those that a mesh axis runs over, the one named last changes fastest.
Arguments:
- fine_nodes: float32 [8, 3, 4, 128, 32, 256], P('tm', None, None, 'space'), may hold values from -5 to 5
- heating: float32 [128, 32, 256], P('space'), may hold values from -4 to 4
Outputs:
- next_nodes: float32 [8, 3, 4, 128, 32, 256], P('tm', None, None, 'space')
The draws below stay inside these ranges and needn't reach their ends.
All inputs are finite; a program needn't handle non-finite values.
Results may differ from the reference program's by a relative error of at most 0.0001.
Values sent between devices are 32-bit elements; how exact they have to be, the bound alone decides.
No kernel may reach another device: no remote copies, remote signals or barrier semaphores. Data moves between devices by JAX's collectives and lax.ppermute only.
A program may use at most 128 MiB of HBM per device.

```python
import jax
import jax.numpy as jnp
from jax import lax

NY = 32
NX = 256
SLABS = 8
NZ = 128


def draw_heating(key, part):
    key = jax.random.fold_in(key, 7)
    return jnp.clip(jax.random.normal(key, (NZ, NY, NX), jnp.float32), -4.0, 4.0)


def steps_of(rng, extent, shards, smallest, largest):
    def one(dim, parts):
        heights = jax.random.uniform(jax.random.fold_in(jax.random.fold_in(rng, 6), dim), (parts,), jnp.float32, smallest / len(shards), largest / len(shards))
        return jnp.repeat(jnp.exp(heights), extent[dim] // parts).reshape((-1,) + (1,) * (len(extent) - dim - 1))

    loudness = one(*shards[0])
    for cut in shards[1:]:
        loudness = loudness * one(*cut)
    return loudness


def gaussian(stream_key, extent, deviation, limit, shards=(), kind=jnp.bfloat16):
    array = jax.random.normal(stream_key, extent, jnp.float32) * deviation
    if len(shards) > 0:
        array = steps_of(stream_key, extent, shards, -0.22, 0.18) * array
    return jnp.clip(array, min=-limit, max=limit).astype(kind)


def setup_inputs(seed: int = 0) -> dict:
    key_list = jax.random.split(jax.random.key(seed), 3)
    fine_nodes = gaussian(key_list[0], (SLABS, 3, 4, NZ, NY, NX), 1.0, 5.0, ((0, 8), (3, 16)), jnp.float32)
    heating = draw_heating(jax.random.fold_in(key_list[2], 71), 0)
    return {"fine_nodes": fine_nodes, "heating": heating}


ROTATION = 2.0
VISCOSITY = 0.4
DIFFUSIVITY = 0.3
STRATIFICATION = 1.0
SLAB_TIME = 0.25
HALF_TIME = 0.125
EDGE_WEIGHT = 5.0 / 24.0
MIDDLE_WEIGHT = 1.0 / 3.0
FAR_WEIGHT = -1.0 / 24.0
SIXTH = 1.0 / 6.0
TWO_THIRDS = 2.0 / 3.0


def laplacian(widened, spacing):
    centre = widened[..., 2:-2, :, :]
    depth_part = 16.0 * (widened[..., 1:-3, :, :] + widened[..., 3:-1, :, :]) - (widened[..., :-4, :, :] + widened[..., 4:, :, :]) - 30.0 * centre
    across = 16.0 * (jnp.roll(centre, 1, -2) + jnp.roll(centre, -1, -2)) - (jnp.roll(centre, 2, -2) + jnp.roll(centre, -2, -2)) - 30.0 * centre
    along_part = 16.0 * (jnp.roll(centre, 1, -1) + jnp.roll(centre, -1, -1)) - (jnp.roll(centre, 2, -1) + jnp.roll(centre, -2, -1)) - 30.0 * centre
    return (depth_part + across + along_part) * (1.0 / (12.0 * spacing * spacing))


def tendency(widened, source, spacing):
    laplace = laplacian(widened, spacing)
    centre = widened[..., 2:-2, :, :]
    east_flow = centre[..., 0, :, :, :]
    north_flow = centre[..., 1, :, :, :]
    upward = centre[..., 2, :, :, :]
    buoyancy = centre[..., 3, :, :, :]
    return jnp.stack([
        ROTATION * north_flow + VISCOSITY * laplace[..., 0, :, :, :],
        -ROTATION * east_flow + VISCOSITY * laplace[..., 1, :, :, :],
        buoyancy + VISCOSITY * laplace[..., 2, :, :, :],
        STRATIFICATION * upward + DIFFUSIVITY * laplace[..., 3, :, :, :] + source], axis=-4)


def pad_planes(field):
    widths = [(0, 0)] * (field.ndim - 3) + [(2, 2), (0, 0), (0, 0)]
    return jnp.pad(field, widths)


def pair_table(count):
    coarse_index = jnp.arange(count // 2, dtype=jnp.int32)[:, None]
    fine_index = jnp.arange(count, dtype=jnp.int32)[None, :] // 2
    return (coarse_index == fine_index).astype(jnp.float32)


def restrict(field):
    leading_shape = field.shape[:-3]
    depth, rows, columns = field.shape[-3:]
    planes = field.reshape(leading_shape + (depth // 2, 2, rows, columns))
    halved = jnp.sum(planes, axis=-3) * 0.5
    row_table = pair_table(rows) * 0.5
    column_table = pair_table(columns) * 0.5
    halved = jnp.einsum("pr,...rc->...pc", row_table, halved, precision=lax.Precision.HIGHEST)
    return jnp.dot(halved, column_table.T, precision=lax.Precision.HIGHEST)


def prolong(field):
    rows, columns = field.shape[-2:]
    row_table = pair_table(2 * rows)
    column_table = pair_table(2 * columns)
    spread = jnp.repeat(field, 2, -3)
    spread = jnp.einsum("pr,...pc->...rc", row_table, spread, precision=lax.Precision.HIGHEST)
    return jnp.dot(spread, column_table, precision=lax.Precision.HIGHEST)


def fine_part(node_values, heating, coarse_heat):
    slopes = tendency(pad_planes(node_values), heating, 1.0)
    first_node = node_values[0] + SLAB_TIME * (EDGE_WEIGHT * slopes[0] + MIDDLE_WEIGHT * slopes[1] + FAR_WEIGHT * slopes[2])
    first_slope = tendency(pad_planes(first_node), heating, 1.0)
    second_node = first_node + HALF_TIME * (first_slope - slopes[1]) + SLAB_TIME * (FAR_WEIGHT * slopes[0] + MIDDLE_WEIGHT * slopes[1] + EDGE_WEIGHT * slopes[2])
    second_slope = tendency(pad_planes(second_node), heating, 1.0)
    fine_sum = SLAB_TIME * (SIXTH * slopes[0] + TWO_THIRDS * first_slope + SIXTH * second_slope)
    coarse_first = restrict(node_values[0])
    coarse_last = restrict(second_node)
    coarse_slopes = tendency(pad_planes(jnp.stack([coarse_first, coarse_last])), coarse_heat, 2.0)
    correction = restrict(fine_sum) - HALF_TIME * (coarse_slopes[0] + coarse_slopes[1])
    rest = -SLAB_TIME * coarse_slopes[0] + HALF_TIME * (coarse_slopes[0] + coarse_slopes[1]) + correction
    return first_node, second_node, coarse_first, coarse_last, rest, correction


def coarse_sweeps(coarse_start, rest, correction, coarse_heat):
    slope_start = tendency(pad_planes(coarse_start), coarse_heat, 2.0)
    middle = coarse_start + SLAB_TIME * slope_start + rest
    slope_middle = tendency(pad_planes(middle), coarse_heat, 2.0)
    return coarse_start + HALF_TIME * (slope_start + slope_middle) + correction


def reference(fine_nodes, heating):
    coarse_heat = restrict(heating)

    def per_slab(node_values):
        return fine_part(node_values, heating, coarse_heat)

    firsts, seconds, coarse_firsts, coarse_lasts, rests, corrections = lax.map(per_slab, fine_nodes)
    starts = []
    finishes = []
    coarse_start = coarse_firsts[0]
    for slab_index in range(SLABS):
        if slab_index > 0:
            coarse_start = finishes[-1]
        finish = coarse_sweeps(coarse_start, rests[slab_index], corrections[slab_index], coarse_heat)
        starts.append(coarse_start)
        finishes.append(finish)
    results = []
    previous = fine_nodes[0, 0]
    for slab_index in range(SLABS):
        middle = firsts[slab_index] + prolong(0.5 * ((starts[slab_index] - coarse_firsts[slab_index]) + (finishes[slab_index] - coarse_lasts[slab_index])))
        last_node = seconds[slab_index] + prolong(finishes[slab_index] - coarse_lasts[slab_index])
        results.append(jnp.stack([previous, middle, last_node]))
        previous = last_node
    return jnp.stack(results)
```

```python
import numpy as np
import jax
import jax.numpy as jnp
from jax import lax
from jax.experimental import pallas as pl
from jax.experimental.pallas import tpu as pltpu
from jax.sharding import PartitionSpec as P

VISCOSITY = 0.4
DIFFUSIVITY = 0.3
SLAB_TIME = 0.25
HALF_TIME = 0.125

SLABS = 8
BLOCKS = 16
NZ, NY, NX = 128, 32, 256
CZ, CY, CX = NZ // 2, NY // 2, NX // 2
FINE = NZ // BLOCKS
COARSE = CZ // BLOCKS
CHUNK = CX // SLABS
SPILL = 5
AXES = ("tm", "space")
F32 = jnp.float32
BF16 = jnp.bfloat16


def real_basis(count):
    j = np.arange(count)
    rows, values = [], []
    for k in range(count):
        theta = 2.0 * np.pi * k / count
        if k == 0:
            row = np.ones(count)
        elif 2 * k == count:
            row = np.cos(np.pi * j)
        elif 2 * k < count:
            row = np.cos(theta * j) * np.sqrt(2.0)
        else:
            row = np.sin(theta * j) * np.sqrt(2.0)
        rows.append(row / np.sqrt(count))
        values.append((32.0 * np.cos(theta) - 2.0 * np.cos(2.0 * theta) - 30.0) / 48.0)
    return np.array(rows), np.array(values)


def pairs(count):
    return np.repeat(np.eye(count), 2, axis=0)


def circulant(count):
    eye = np.eye(count)
    return (
        16.0 * (np.roll(eye, 1, 0) + np.roll(eye, -1, 0))
        - (np.roll(eye, 2, 0) + np.roll(eye, -2, 0))
        - 30.0 * eye
    )


def split(matrix):
    matrix = np.asarray(matrix, np.float32)
    high = matrix.astype(jnp.bfloat16)
    low = (matrix - high.astype(np.float32)).astype(jnp.bfloat16)
    return np.stack([high, low])


FY, LAM_Y = real_basis(CY)
FX, LAM_X = real_basis(CX)


def depth_basis():
    eye = np.eye(CZ)
    band = -30.0 * eye
    for offset, weight in ((1, 16.0), (2, -1.0)):
        band += weight * (np.eye(CZ, k=offset) + np.eye(CZ, k=-offset))
    values, vectors = np.linalg.eigh(band / 48.0)
    return values, vectors


LAM_Z, QZ = depth_basis()

DOWN_Y = FY @ pairs(CY).T * 0.5
DOWN_YL = DOWN_Y @ circulant(NY)
DOWN_X = (FX @ pairs(CX).T * 0.5).T
DOWN_XL = circulant(NX) @ DOWN_X
UP_Y = pairs(CY) @ FY.T
UP_X = FX @ pairs(CX).T

K10 = split(np.kron(np.eye(10), DOWN_Y))
K8 = split(np.kron(np.eye(8), DOWN_Y))
K8L = split(np.kron(np.eye(8), DOWN_YL))
K4 = split(np.kron(np.eye(4), DOWN_Y))
X0 = split(DOWN_X)
X1 = split(DOWN_XL)
LAM_XY = (LAM_Y[:, None] + LAM_X[None, :]).astype(np.float32)


def depth_forward():
    table = np.zeros((2, CZ, BLOCKS, 8))
    for half in range(2):
        for block in range(BLOCKS):
            for slot in range(8):
                z = block * COARSE + half * 8 + slot - SPILL
                if 0 <= z < CZ:
                    table[half, :, block, slot] = QZ[z]
    return table.reshape(2 * CZ, BLOCKS * 8)


ZF = split(depth_forward())
ZB = split(QZ)


def up_y_table():
    table = np.zeros((COARSE, NY, CY, COARSE))
    for z in range(COARSE):
        table[z, :, :, z] = UP_Y
    return table.reshape(COARSE * NY, CY * COARSE)


YB = split(up_y_table())
XB = split(UP_X)


def mode_values():
    table = np.zeros((SLABS, BLOCKS, 2, 4, CHUNK))
    for t in range(SLABS):
        for p in range(BLOCKS):
            table[t, p] = LAM_Y[p] + LAM_X[t * CHUNK:(t + 1) * CHUNK]
    return table.reshape(SLABS * BLOCKS, 128).astype(np.float32)


def lane_constants():
    own = np.array([VISCOSITY, VISCOSITY, VISCOSITY, DIFFUSIVITY])
    partner = np.array([VISCOSITY, VISCOSITY, DIFFUSIVITY, VISCOSITY])
    couple = np.array([2.0, -2.0, 1.0, 1.0])
    product = np.array([-4.0, -4.0, 1.0, 1.0])
    table = np.zeros((8, 2, 4, CHUNK))
    for row, values in enumerate((own, partner, couple, product)):
        table[row] = values[None, :, None]
    return table.reshape(8, 128).astype(np.float32)


MODE_XY = mode_values()
LANES = lane_constants()
LAM_Z_COLUMN = np.repeat(LAM_Z[:, None], 128, axis=1).astype(np.float32)


def halves(x):
    high = x.astype(BF16)
    return high, (x - high.astype(F32)).astype(BF16)


def dot(a, b):
    return jnp.dot(a, b, preferred_element_type=F32)


def left(table, x):
    high, low = halves(x)
    return dot(table[0], high) + (dot(table[0], low) + dot(table[1], high))


def right(x, table):
    high, low = halves(x)
    return dot(high, table[0]) + (dot(low, table[0]) + dot(high, table[1]))


def rolled(x, by, axis):
    return pltpu.roll(x, by % x.shape[axis], axis)


def lateral(x):
    near = rolled(x, 1, 0) + rolled(x, -1, 0) + (rolled(x, 1, 1) + rolled(x, -1, 1))
    far = rolled(x, 2, 0) + rolled(x, -2, 0) + (rolled(x, 2, 1) + rolled(x, -2, 1))
    return 16.0 * near - far


def total(terms):
    out = terms[0]
    for term in terms[1:]:
        out = out + term
    return out


def chunk_transpose(values):
    values = list(values)
    lane = lax.broadcasted_iota(jnp.int32, values[0].shape, 1)
    for bit in (1, 2, 4):
        shift = CHUNK * bit
        low = (lane & shift) == 0
        for i in range(8):
            if i & bit:
                continue
            j = i | bit
            first, second = values[i], values[j]
            values[i] = jnp.where(low, first, rolled(second, shift, 1))
            values[j] = jnp.where(low, rolled(first, -shift, 1), second)
    return values


def field_scalars(f):
    nu = jnp.where(f == 3, DIFFUSIVITY, VISCOSITY).astype(F32)
    couple = jnp.where(f == 0, 2.0, jnp.where(f == 1, -2.0, 1.0)).astype(F32)
    heated = jnp.where(f == 3, 1.0, 0.0).astype(F32)
    partner = f + 1 - 2 * (f % 2)
    return nu, couple, heated, partner


def fine_kernel(flags, u, q, k10, k8, k8l, k4, x0, x1, lam,
                first_out, second_out, up_out, down_out, send_out,
                a_s, fe, be, se, cs, w_s, v_s, y_s, g_s):
    mu, keep_low, keep_high = flags[0], flags[1], flags[2]

    def kept(value, p, count):
        if p < 0:
            return value * keep_low
        if p >= count:
            return value * keep_high
        return value

    def combine(f, _):
        for p in range(FINE):
            a_s[f, p] = (5.0 / 24.0) * u[0, f, p] + (1.0 / 3.0) * u[1, f, p] - (1.0 / 24.0) * u[2, f, p]
        return 0

    lax.fori_loop(0, 4, combine, 0)

    def depth_terms(ref, f, p, low, high, base):
        near = [ref[f, p + o + base] for o in (-1, 1) if low <= p + o < high]
        far = [ref[f, p + o + base] for o in (-2, 2) if low <= p + o < high]
        out = None
        if near:
            out = 16.0 * total(near)
        if far:
            out = -total(far) if out is None else out - total(far)
        return out

    def first_stage(f, _):
        nu, couple, heated, partner = field_scalars(f)
        scale = nu * (SLAB_TIME / 12.0)
        for p in range(-2, FINE + 2):
            acc = depth_terms(a_s, f, p, 0, FINE, 0)
            if 0 <= p < FINE:
                centre = a_s[f, p]
                acc = acc + (lateral(centre) - 90.0 * centre)
                value = (scale * acc + (couple * SLAB_TIME) * a_s[partner, p]
                         + (u[0, f, p] + (heated * HALF_TIME) * q[p]))
                rest = (-1.0 / 24.0) * u[0, f, p] - (1.0 / 6.0) * u[1, f, p] + (5.0 / 24.0) * u[2, f, p]
                fe[f, p + 2] = value
                be[f, p + 2] = 0.5 * value + rest
                first_out[f, p] = value
            else:
                value = kept(scale * acc, p, FINE)
                fe[f, p + 2] = value
                be[f, p + 2] = 0.5 * value
                if p < 0:
                    down_out[p + 2, f] = value
                else:
                    up_out[p - FINE, f] = value
        return 0

    lax.fori_loop(0, 4, first_stage, 0)

    def second_stage(f, _):
        nu, couple, heated, partner = field_scalars(f)
        scale = nu * (SLAB_TIME / 12.0)
        for p in range(-4, FINE + 4):
            acc = depth_terms(be, f, p, -2, FINE + 2, 2)
            if -2 <= p < FINE + 2:
                centre = be[f, p + 2]
                acc = acc + (lateral(centre) - 90.0 * centre)
                value = scale * acc + (couple * SLAB_TIME) * be[partner, p + 2] + fe[f, p + 2]
                if 0 <= p < FINE:
                    value = value + (heated * HALF_TIME) * q[p]
            else:
                value = scale * acc
            value = kept(value, p, FINE)
            se[f, p + 4] = value
            c = (1.0 / 6.0) * value
            if -2 <= p < FINE + 2:
                c = c + (2.0 / 3.0) * fe[f, p + 2]
            if 0 <= p < FINE:
                c = c + (1.0 / 6.0) * u[0, f, p]
                second_out[f, p] = value
            elif p < 0:
                down_out[p + 6, f] = value
            else:
                up_out[p - FINE + 2, f] = value
            cs[f, p + 4] = c
        return 0

    lax.fori_loop(0, 4, second_stage, 0)

    def coarse_loop(f, _):
        nu, couple, heated, partner = field_scalars(f)
        scale = nu * (SLAB_TIME / 12.0)
        mean, last, start, defect = [], [], [], []
        for k in range(-2, COARSE + 2):
            mean.append(0.5 * (cs[f, 2 * k + 4] + cs[f, 2 * k + 5]))
            last.append(0.5 * (se[f, 2 * k + 4] + se[f, 2 * k + 5]))
        for k in range(COARSE):
            start.append(0.5 * (u[0, f, 2 * k] + u[0, f, 2 * k + 1]))
        for k in range(-3, COARSE + 3):
            value = None
            for weight, ps in ((-7.0, (2 * k, 2 * k + 1)), (7.5, (2 * k - 1, 2 * k + 2)), (-0.5, (2 * k - 2, 2 * k + 3))):
                part = [cs[f, p + 4] for p in ps if -4 <= p < FINE + 4]
                if part:
                    part = weight * total(part)
                    value = part if value is None else value + part
            value = scale * value
            if -2 <= k < COARSE + 2:
                value = value + (couple * (SLAB_TIME * 0.5)) * (cs[partner, 2 * k + 4] + cs[partner, 2 * k + 5])
            if 0 <= k < COARSE:
                value = value + (heated * (SLAB_TIME * 0.5)) * (q[2 * k] + q[2 * k + 1])
            value = kept(value, k, COARSE)
            if -2 <= k < COARSE + 2:
                value = value - last[k + 2]
            if 0 <= k < COARSE:
                value = value + start[k]
            defect.append(value)
        for k in range(COARSE):
            last[k + 2] = last[k + 2] - mu * start[k]
        c_rows = jnp.concatenate(mean, axis=0)
        c_y = left(k8, c_rows)
        c_yl = left(k8l, c_rows)
        w_y = left(k10, jnp.concatenate(defect, axis=0))
        v_y = left(k8, jnp.concatenate(last, axis=0))
        s_y = left(k4, jnp.concatenate(start, axis=0))
        w_s[f] = right(w_y, x0)
        c_hat = scale * (right(c_y, x1) + right(c_yl, x0))
        w_s[f, pl.ds(CY, 8 * CY)] = w_s[f, pl.ds(CY, 8 * CY)] + c_hat
        v_s[f] = right(v_y, x0)
        y_s[f] = right(s_y, x0)
        return 0

    lax.fori_loop(0, 4, coarse_loop, 0)

    lam_xy = lam[...]

    def plane(ref, f, k, low, high):
        if low <= k < high:
            return ref[f, pl.ds((k - low) * CY, CY)]
        return None

    def coarse_slope(ref, f, k, low, high):
        nu, couple, _, partner = field_scalars(f)
        out = None
        for weight, offsets in ((16.0 / 48.0, (-1, 1)), (-1.0 / 48.0, (-2, 2))):
            part = [plane(ref, f, k + o, low, high) for o in offsets]
            part = [value for value in part if value is not None]
            if part:
                part = weight * total(part)
                out = part if out is None else out + part
        centre = plane(ref, f, k, low, high)
        if centre is None:
            return nu * out
        out = out + (lam_xy - 30.0 / 48.0) * centre
        return nu * out + couple * plane(ref, partner, k, low, high)

    def defect_loop(f, _):
        for k in range(-2, COARSE + 2):
            value = coarse_slope(y_s, f, k, 0, COARSE)
            value = kept((mu * SLAB_TIME) * value, k, COARSE)
            rows = pl.ds((k + 3) * CY, CY)
            w_s[f, rows] = w_s[f, rows] - value
        return 0

    lax.fori_loop(0, 4, defect_loop, 0)

    def packet_loop(f, _):
        for k in range(-SPILL, 16 - SPILL):
            rows = pl.ds((k + SPILL) * CY, CY)
            if k >= COARSE + SPILL:
                g_s[f, rows] = jnp.zeros((CY, CX), F32)
                continue
            value = kept(HALF_TIME * coarse_slope(w_s, f, k, -3, COARSE + 3), k, COARSE)
            for part in (plane(w_s, f, k, -3, COARSE + 3), plane(v_s, f, k, -2, COARSE + 2)):
                if part is not None:
                    value = value + part
            g_s[f, rows] = value
        return 0

    lax.fori_loop(0, 4, packet_loop, 0)

    def pack(p, _):
        values = []
        for half in range(2):
            for f in range(4):
                values.append(g_s[f, pl.ds(half * 8 * CY + p, 8, stride=CY), :])
        for t, value in enumerate(chunk_transpose(values)):
            send_out[t * BLOCKS + p] = value
        return 0

    lax.fori_loop(0, BLOCKS, pack, 0)


def mode_kernel(g, lam_xy, lam_z, lanes, zf, zb, out):
    lam = lam_z[...] + lam_xy[...]
    nu, other, couple, product = (lanes[pl.ds(i, 1)] for i in range(4))
    own = nu * lam
    partner = other * lam
    half_square = 0.5 * SLAB_TIME * SLAB_TIME
    diagonal = 1.0 + SLAB_TIME * own + half_square * (own * own + product)
    mixing = couple * (SLAB_TIME + half_square * (own + partner))
    lane = lax.broadcasted_iota(jnp.int32, (CZ, 128), 1)
    even = (lane & CHUNK) == 0
    left_half = lane < 64

    rows = BLOCKS * 8
    state = None
    states = [jnp.zeros((CZ, 128), F32)]
    for s in range(SLABS):
        both = left(zf, g[pl.ds(s * rows, rows)])
        source = both[:CZ] + rolled(both[CZ:], 64, 1)
        if state is None:
            state = source
        else:
            swapped = jnp.where(even, rolled(state, -CHUNK, 1), rolled(state, CHUNK, 1))
            state = diagonal * state + mixing * swapped + source
        state = jnp.where(left_half, state, 0.0)
        states.append(state)
    for s in range(SLABS):
        packed = states[s] + rolled(states[s + 1], 64, 1)
        out[pl.ds(s * CZ, CZ)] = left(zb, packed)


def paired(x, axis):
    index = lax.broadcasted_iota(jnp.int32, x.shape, axis)
    return x + jnp.where((index & 1) == 0, rolled(x, -1, axis), rolled(x, 1, axis))


def join_kernel(flags, first_c, second_c, low, high, u, first_out, second_out):
    mu = flags[0]

    def body(f, _):
        firsts, seconds = [], []
        for p in range(FINE):
            first = first_c[f, p]
            second = second_c[f, p]
            if p < 2:
                first = first + low[p, f]
            if p >= FINE - 2:
                first = first + high[p - FINE + 2, f]
            if p < 4:
                second = second + low[2 + p, f]
            else:
                second = second + high[2 + p - 4, f]
            firsts.append(first)
            seconds.append(second)
        for k in range(COARSE):
            last = paired(paired(0.125 * (seconds[2 * k] + seconds[2 * k + 1]), 0), 1)
            start = paired(paired((0.125 * mu) * (u[0, f, 2 * k] + u[0, f, 2 * k + 1]), 0), 1)
            middle = 0.5 * (last + start)
            for p in (2 * k, 2 * k + 1):
                first_out[f, p] = firsts[p] - middle
                second_out[f, p] = seconds[p] - last
        return 0

    lax.fori_loop(0, 4, body, 0)


def last_kernel(flags, modes, first, second, before, u, yb, xb, out, h_s):
    leading = 1.0 - flags[0]
    for r in range(8):
        values = [modes[pl.ds(t * 64 + r * 8, 8)] for t in range(SLABS)]
        for g, value in enumerate(chunk_transpose(values)):
            h_s[g, pl.ds(r * 8, 8)] = value

    def body(f, _):
        start = right(left(yb, h_s[f]), xb)
        end = right(left(yb, h_s[4 + f]), xb)
        middle = 0.5 * (start + end)
        for p in range(FINE):
            rows = slice((p // 2) * NY, (p // 2 + 1) * NY)
            out[0, f, p] = before[f, p] + start[rows] + leading * u[0, f, p]
            out[1, f, p] = first[f, p] + middle[rows]
            out[2, f, p] = second[f, p] + end[rows]
        return 0

    lax.fori_loop(0, 4, body, 0)


VM = pl.BlockSpec(memory_space=pltpu.VMEM)
SM = pl.BlockSpec(memory_space=pltpu.SMEM)
NODE0 = pl.BlockSpec((1, 4, FINE, NY, NX), lambda i: (0, 0, 0, 0, 0))


def params(mib):
    return pltpu.CompilerParams(vmem_limit_bytes=mib << 20)


def shape(*sizes):
    return jax.ShapeDtypeStruct(sizes, F32)


def per_device(fine_nodes, heating):
    u = fine_nodes[0]
    tm = lax.axis_index("tm")
    space = lax.axis_index("space")
    flags = jnp.stack([tm > 0, space > 0, space < BLOCKS - 1, space < 0]).astype(F32)
    field = (4, FINE, NY, NX)
    spill = (6, 4, NY, NX)

    with jax.named_scope("fine"):
        first_c, second_c, up, down, packet = pl.pallas_call(
            fine_kernel,
            out_shape=[shape(*field), shape(*field), shape(*spill), shape(*spill), shape(SLABS * BLOCKS, 8, 128)],
            in_specs=[SM] + [VM] * 9,
            out_specs=[VM] * 5,
            scratch_shapes=[
                pltpu.VMEM(field, F32),
                pltpu.VMEM((4, FINE + 4, NY, NX), F32),
                pltpu.VMEM((4, FINE + 4, NY, NX), F32),
                pltpu.VMEM((4, FINE + 8, NY, NX), F32),
                pltpu.VMEM((4, FINE + 8, NY, NX), F32),
                pltpu.VMEM((4, 10 * CY, CX), F32),
                pltpu.VMEM((4, 8 * CY, CX), F32),
                pltpu.VMEM((4, 4 * CY, CX), F32),
                pltpu.VMEM((4, 16 * CY, CX), F32),
            ],
            compiler_params=params(48),
        )(flags, u, heating, K10, K8, K8L, K4, X0, X1, LAM_XY)

    with jax.named_scope("to_modes"):
        modes = lax.all_to_all(packet, AXES, 0, 0, tiled=True)

    with jax.named_scope("spill"):
        low = lax.ppermute(up, "space", [(i, i + 1) for i in range(BLOCKS - 1)])
        high = lax.ppermute(down, "space", [(i + 1, i) for i in range(BLOCKS - 1)])

    with jax.named_scope("join"):
        first, second = pl.pallas_call(
            join_kernel,
            grid=(1,),
            out_shape=[shape(*field), shape(*field)],
            in_specs=[SM] + [VM] * 4 + [NODE0],
            out_specs=[VM] * 2,
            compiler_params=params(32),
        )(flags, first_c, second_c, low, high, u)

    with jax.named_scope("pass"):
        before = lax.ppermute(second, "tm", [(i, i + 1) for i in range(SLABS - 1)])

    with jax.named_scope("modes"):
        lam_xy = lax.dynamic_slice(jnp.asarray(MODE_XY), (tm * BLOCKS + space, 0), (1, 128))
        solved = pl.pallas_call(
            mode_kernel,
            out_shape=shape(SLABS * CZ, 128),
            in_specs=[VM] * 6,
            out_specs=VM,
            compiler_params=params(16),
        )(modes.reshape(SLABS * BLOCKS * 8, 128), lam_xy, LAM_Z_COLUMN, LANES, ZF, ZB)

    with jax.named_scope("from_modes"):
        solved = solved.reshape(SLABS * BLOCKS, COARSE, 128)
        back = lax.all_to_all(solved, AXES, 0, 0, tiled=True).reshape(SLABS * CZ, 128)

    with jax.named_scope("last"):
        out = pl.pallas_call(
            last_kernel,
            grid=(1,),
            out_shape=shape(3, *field),
            in_specs=[SM] + [VM] * 4 + [NODE0] + [VM] * 2,
            out_specs=VM,
            scratch_shapes=[pltpu.VMEM((8, 64, 128), F32)],
            compiler_params=params(32),
        )(flags, back, first, second, before, u, YB, XB)
    return out[None]


def solution(mesh):
    in_specs = (P("tm", None, None, "space", None, None), P("space", None, None))
    out_specs = P("tm", None, None, "space", None, None)
    return jax.shard_map(
        per_device, mesh=mesh, in_specs=in_specs, out_specs=out_specs, check_vma=False
    )
```

```python
import numpy as np
import jax
import jax.numpy as jnp
from jax import lax
from jax.experimental import pallas as pl
from jax.experimental.pallas import tpu as pltpu
from jax.sharding import PartitionSpec as P

VISCOSITY = 0.4
DIFFUSIVITY = 0.3
SLAB_TIME = 0.25
HALF_TIME = 0.125

SLABS = 8
BLOCKS = 16
NZ, NY, NX = 128, 32, 256
CZ, CY, CX = NZ // 2, NY // 2, NX // 2
FINE = NZ // BLOCKS
COARSE = CZ // BLOCKS
CHUNK = CX // SLABS
SPILL = 5
AXES = ("tm", "space")
F32 = jnp.float32
BF16 = jnp.bfloat16


def real_basis(count):
    j = np.arange(count)
    rows, values = [], []
    for k in range(count):
        theta = 2.0 * np.pi * k / count
        if k == 0:
            row = np.ones(count)
        elif 2 * k == count:
            row = np.cos(np.pi * j)
        elif 2 * k < count:
            row = np.cos(theta * j) * np.sqrt(2.0)
        else:
            row = np.sin(theta * j) * np.sqrt(2.0)
        rows.append(row / np.sqrt(count))
        values.append((32.0 * np.cos(theta) - 2.0 * np.cos(2.0 * theta) - 30.0) / 48.0)
    return np.array(rows), np.array(values)


def pairs(count):
    return np.repeat(np.eye(count), 2, axis=0)


def circulant(count):
    eye = np.eye(count)
    return (
        16.0 * (np.roll(eye, 1, 0) + np.roll(eye, -1, 0))
        - (np.roll(eye, 2, 0) + np.roll(eye, -2, 0))
        - 30.0 * eye
    )


def split(matrix):
    matrix = np.asarray(matrix, np.float32)
    high = matrix.astype(jnp.bfloat16)
    low = (matrix - high.astype(np.float32)).astype(jnp.bfloat16)
    return np.stack([high, low])


FY, LAM_Y = real_basis(CY)
FX, LAM_X = real_basis(CX)


def depth_basis():
    eye = np.eye(CZ)
    band = -30.0 * eye
    for offset, weight in ((1, 16.0), (2, -1.0)):
        band += weight * (np.eye(CZ, k=offset) + np.eye(CZ, k=-offset))
    values, vectors = np.linalg.eigh(band / 48.0)
    return values, vectors


LAM_Z, QZ = depth_basis()

DOWN_Y = FY @ pairs(CY).T * 0.5
DOWN_YL = DOWN_Y @ circulant(NY)
DOWN_X = (FX @ pairs(CX).T * 0.5).T
DOWN_XL = circulant(NX) @ DOWN_X
UP_Y = pairs(CY) @ FY.T
UP_X = FX @ pairs(CX).T


def depth_table(outs, out_low, ins, in_low):
    table = np.zeros((outs, ins))
    for row in range(outs):
        for column in range(ins):
            offset = abs(row + out_low - column - in_low)
            table[row, column] = {0: -30.0, 1: 16.0, 2: -1.0}.get(offset, 0.0)
    return table


def same_plane(outs, out_low, ins, in_low):
    return (np.arange(outs)[:, None] + out_low == np.arange(ins)[None, :] + in_low).astype(np.float64)


def mean_table(outs, out_low, ins, in_low):
    return 0.5 * (np.arange(outs)[:, None] + out_low == (np.arange(ins)[None, :] + in_low) // 2)


def exact(matrix):
    high = np.asarray(matrix, np.float32).astype(jnp.bfloat16)
    assert np.array_equal(high.astype(np.float64), matrix)
    return high


def stacked(matrix):
    return split(matrix).reshape(-1, matrix.shape[1])


EYE_Y = np.eye(NY)
STEP1 = exact(np.kron(depth_table(12, -2, 8, 0), EYE_Y) + np.kron(same_plane(12, -2, 8, 0), circulant(NY)))
STEP2 = exact(np.kron(depth_table(16, -4, 12, -2), EYE_Y) + np.kron(same_plane(16, -4, 12, -2), circulant(NY)))
ALONG = exact(circulant(NX))
MEAN_C = np.kron(mean_table(8, -2, 16, -4), DOWN_Y)
MEAN_L = (
    np.kron(mean_table(10, -3, 20, -6) @ depth_table(20, -6, 16, -4), DOWN_Y)
    + np.kron(mean_table(10, -3, 16, -4), DOWN_YL)
)
DOWN_C = stacked(np.concatenate([MEAN_L, MEAN_C]))
DOWN_S = stacked(MEAN_C)
DOWN_U = stacked(np.kron(mean_table(4, 0, 8, 0), DOWN_Y))
X0 = split(DOWN_X)
X1 = split(DOWN_XL)
LAM_XY = (LAM_Y[:, None] + LAM_X[None, :]).astype(np.float32)


def depth_forward():
    table = np.zeros((2, CZ, BLOCKS, 8))
    for half in range(2):
        for block in range(BLOCKS):
            for slot in range(8):
                z = block * COARSE + half * 8 + slot - SPILL
                if 0 <= z < CZ:
                    table[half, :, block, slot] = QZ[z]
    return table.reshape(2 * CZ, BLOCKS * 8)


ZF = split(depth_forward())
ZB = split(QZ)


def up_y_table():
    table = np.zeros((COARSE, NY, CY, COARSE))
    for z in range(COARSE):
        table[z, :, :, z] = UP_Y
    return table.reshape(COARSE * NY, CY * COARSE)


YB = split(up_y_table())
XB = split(UP_X)


def mode_values():
    table = np.zeros((SLABS, BLOCKS, 2, 4, CHUNK))
    for t in range(SLABS):
        for p in range(BLOCKS):
            table[t, p] = LAM_Y[p] + LAM_X[t * CHUNK:(t + 1) * CHUNK]
    return table.reshape(SLABS * BLOCKS, 128).astype(np.float32)


def lane_constants():
    own = np.array([VISCOSITY, VISCOSITY, VISCOSITY, DIFFUSIVITY])
    partner = np.array([VISCOSITY, VISCOSITY, DIFFUSIVITY, VISCOSITY])
    couple = np.array([2.0, -2.0, 1.0, 1.0])
    product = np.array([-4.0, -4.0, 1.0, 1.0])
    table = np.zeros((8, 2, 4, CHUNK))
    for row, values in enumerate((own, partner, couple, product)):
        table[row] = values[None, :, None]
    return table.reshape(8, 128).astype(np.float32)


MODE_XY = mode_values()
LANES = lane_constants()
LAM_Z_COLUMN = np.repeat(LAM_Z[:, None], 128, axis=1).astype(np.float32)


def halves(x):
    high = x.astype(BF16)
    return high, (x - high.astype(F32)).astype(BF16)


def dot(a, b):
    return jnp.dot(a, b, preferred_element_type=F32)


def left(table, x):
    high, low = halves(x)
    return dot(table[0], high) + (dot(table[0], low) + dot(table[1], high))


def right(x, table):
    high, low = halves(x)
    return dot(high, table[0]) + (dot(low, table[0]) + dot(high, table[1]))


def rolled(x, by, axis):
    return pltpu.roll(x, by % x.shape[axis], axis)


def lateral(x):
    near = rolled(x, 1, 0) + rolled(x, -1, 0) + (rolled(x, 1, 1) + rolled(x, -1, 1))
    far = rolled(x, 2, 0) + rolled(x, -2, 0) + (rolled(x, 2, 1) + rolled(x, -2, 1))
    return 16.0 * near - far


def total(terms):
    out = terms[0]
    for term in terms[1:]:
        out = out + term
    return out


def chunk_transpose(values):
    values = list(values)
    lane = lax.broadcasted_iota(jnp.int32, values[0].shape, 1)
    for bit in (1, 2, 4):
        shift = CHUNK * bit
        low = (lane & shift) == 0
        for i in range(8):
            if i & bit:
                continue
            j = i | bit
            first, second = values[i], values[j]
            values[i] = jnp.where(low, first, rolled(second, shift, 1))
            values[j] = jnp.where(low, rolled(first, -shift, 1), second)
    return values


def left_stacked(table, x):
    high, low = halves(x)
    rows = table.shape[0] // 2
    both = dot(table, high)
    return both[:rows] + (both[rows:] + dot(table[:rows], low))


PLANE = NY
OWN = FINE * PLANE


def fine_kernel(flags, u_hbm, q_hbm, step1_hbm, step2_hbm, along_hbm, down_c_hbm, down_s_hbm, down_u_hbm, x0_hbm, x1_hbm, lam_hbm,
                first_hbm, second_hbm, up_hbm, down_hbm, send_hbm,
                u, q, step1, step2, along, down_c, down_s, down_u, x0, x1, lam,
                a_s, fe, be, se, wy_s, vy_s, cy_s, w_s, v_s, y_s, g_s, send_s, in_sem, u_sem, out_sem, send_sem):
    mu, keep_low, keep_high = flags[0], flags[1], flags[2]
    loads = [
        pltpu.make_async_copy(source, target, in_sem.at[i])
        for i, (source, target) in enumerate((
            (step1_hbm, step1), (along_hbm, along), (q_hbm, q), (step2_hbm, step2), (down_c_hbm, down_c),
            (down_s_hbm, down_s), (down_u_hbm, down_u), (x0_hbm, x0), (x1_hbm, x1), (lam_hbm, lam)))
    ]
    node_loads = [
        [pltpu.make_async_copy(u_hbm.at[n, f], u.at[n, f], u_sem.at[n, f]) for n in range(3)] for f in range(4)
    ]
    for load in node_loads[0] + node_loads[1] + loads + node_loads[2] + node_loads[3]:
        load.start()

    edge = 2 * PLANE
    middle = pl.ds(edge, OWN)
    stores = []

    def store(source, target, sem):
        copy = pltpu.make_async_copy(source, target, sem)
        copy.start()
        stores.append(copy)

    def field(f):
        nu = DIFFUSIVITY if f == 3 else VISCOSITY
        return nu, (2.0, -2.0, 1.0, 1.0)[f], f ^ 1

    def combine(f):
        for load in node_loads[f]:
            load.wait()
        a_s[f] = (5.0 / 24.0) * u[0, f] + (1.0 / 3.0) * u[1, f] - (1.0 / 24.0) * u[2, f]

    def first_stage(f):
        nu, couple, partner = field(f)
        scale = nu * (SLAB_TIME / 12.0)
        high, low = halves(a_s[f])
        column = dot(step1[...], high) + dot(step1[...], low)
        row = dot(high, along[...]) + dot(low, along[...])
        start = u[0, f]
        value = scale * (column[edge:edge + OWN] + row) + (couple * SLAB_TIME) * a_s[partner] + start
        if f == 3:
            value = value + HALF_TIME * q[...]
        fe[f, middle] = value
        be[f, middle] = 0.5 * value + ((-1.0 / 24.0) * start - (1.0 / 6.0) * u[1, f] + (5.0 / 24.0) * u[2, f])
        below = (scale * keep_low) * column[:edge]
        above = (scale * keep_high) * column[edge + OWN:]
        fe[f, pl.ds(0, edge)] = below
        be[f, pl.ds(0, edge)] = 0.5 * below
        fe[f, pl.ds(edge + OWN, edge)] = above
        be[f, pl.ds(edge + OWN, edge)] = 0.5 * above
        store(fe.at[f, middle], first_hbm.at[f], out_sem.at[f, 0])
        store(fe.at[f, pl.ds(0, edge)], down_hbm.at[f, pl.ds(0, edge)], out_sem.at[f, 1])
        store(fe.at[f, pl.ds(edge + OWN, edge)], up_hbm.at[f, pl.ds(0, edge)], out_sem.at[f, 2])

    def second_stage(f, heat_y):
        nu, couple, partner = field(f)
        scale = nu * (SLAB_TIME / 12.0)
        high, low = halves(be[f])
        column = dot(step2[...], high) + dot(step2[...], low)
        row = dot(high, along[...]) + dot(low, along[...])
        first = fe[f]
        value = scale * (column[edge:-edge] + row) + (couple * SLAB_TIME) * be[partner] + first
        centre = value[edge:edge + OWN]
        if f == 3:
            centre = centre + HALF_TIME * q[...]
        below = jnp.concatenate([(scale * keep_low) * column[:edge], keep_low * value[:edge]], axis=0)
        above = jnp.concatenate([keep_high * value[edge + OWN:], (scale * keep_high) * column[-edge:]], axis=0)
        se[f] = jnp.concatenate([below, centre, above], axis=0)
        store(se.at[f, pl.ds(2 * edge, OWN)], second_hbm.at[f], out_sem.at[f, 3])
        store(se.at[f, pl.ds(0, 2 * edge)], down_hbm.at[f, pl.ds(edge, 2 * edge)], out_sem.at[f, 4])
        store(se.at[f, pl.ds(2 * edge + OWN, 2 * edge)], up_hbm.at[f, pl.ds(edge, 2 * edge)], out_sem.at[f, 5])
        c = jnp.concatenate([
            (1.0 / 6.0) * below[:edge],
            (1.0 / 6.0) * below[edge:] + (2.0 / 3.0) * first[:edge],
            (1.0 / 6.0) * (centre + u[0, f]) + (2.0 / 3.0) * first[edge:edge + OWN],
            (1.0 / 6.0) * above[:edge] + (2.0 / 3.0) * first[edge + OWN:],
            (1.0 / 6.0) * above[edge:]], axis=0)
        c_y = left_stacked(down_c[...], c)
        last_y = left_stacked(down_s[...], se[f])
        start_y = left_stacked(down_u[...], u[0, f])
        cy_s[f] = c_y[10 * CY:]
        side = 3 * CY
        own = scale * c_y[side:side + 4 * CY] - last_y[2 * CY:6 * CY] + start_y
        if f == 3:
            own = own + SLAB_TIME * heat_y
        wy_s[f] = jnp.concatenate([
            scale * c_y[:CY],
            scale * c_y[CY:side] - last_y[:2 * CY],
            own,
            scale * c_y[side + 4 * CY:9 * CY] - last_y[6 * CY:],
            scale * c_y[9 * CY:10 * CY]], axis=0)
        vy_s[f, pl.ds(0, 2 * CY)] = last_y[:2 * CY]
        vy_s[f, pl.ds(2 * CY, 4 * CY)] = last_y[2 * CY:6 * CY] - mu * start_y
        vy_s[f, pl.ds(6 * CY, 2 * CY)] = last_y[6 * CY:]
        vy_s[f, pl.ds(8 * CY, 4 * CY)] = start_y

    def across(f):
        nu, couple, partner = field(f)
        scale = nu * (SLAB_TIME / 12.0)
        rows = pl.ds(CY, 8 * CY)
        w_y = wy_s[f]
        mixed = w_y[CY:9 * CY] + (couple * SLAB_TIME) * cy_s[partner]
        w_y = jnp.concatenate([
            keep_low * w_y[:CY], keep_low * mixed[:2 * CY], mixed[2 * CY:6 * CY],
            keep_high * mixed[6 * CY:], keep_high * w_y[9 * CY:]], axis=0)
        w_s[f] = right(w_y, x0)
        w_s[f, rows] = w_s[f, rows] + scale * right(cy_s[f], x1)
        both = right(vy_s[f], x0)
        v_s[f] = both[:8 * CY]
        y_s[f] = both[8 * CY:]

    def kept(value, p, count):
        if p < 0:
            return value * keep_low
        if p >= count:
            return value * keep_high
        return value

    def plane(ref, f, k, low, high):
        if low <= k < high:
            return ref[f, pl.ds((k - low) * CY, CY)]
        return None

    def coarse_slope(ref, f, k, low, high):
        nu, couple, partner = field(f)
        out = None
        for weight, offsets in ((16.0 / 48.0, (-1, 1)), (-1.0 / 48.0, (-2, 2))):
            part = [plane(ref, f, k + o, low, high) for o in offsets]
            part = [value for value in part if value is not None]
            if part:
                part = weight * total(part)
                out = part if out is None else out + part
        centre = plane(ref, f, k, low, high)
        if centre is None:
            return nu * out
        out = out + (lam[...] - 30.0 / 48.0) * centre
        return nu * out + couple * plane(ref, partner, k, low, high)

    def defect(f):
        for k in range(-2, COARSE + 2):
            value = coarse_slope(y_s, f, k, 0, COARSE)
            value = kept((mu * SLAB_TIME) * value, k, COARSE)
            rows = pl.ds((k + 3) * CY, CY)
            w_s[f, rows] = w_s[f, rows] - value

    def packet(f):
        for k in range(-SPILL, 16 - SPILL):
            rows = pl.ds((k + SPILL) * CY, CY)
            if k >= COARSE + SPILL:
                g_s[f, rows] = jnp.zeros((CY, CX), F32)
                continue
            value = kept(HALF_TIME * coarse_slope(w_s, f, k, -3, COARSE + 3), k, COARSE)
            for part in (plane(w_s, f, k, -3, COARSE + 3), plane(v_s, f, k, -2, COARSE + 2)):
                if part is not None:
                    value = value + part
            g_s[f, rows] = value

    for pair in ((0, 1), (2, 3)):
        for f in pair:
            combine(f)
        if pair[0] == 0:
            for load in loads[:3]:
                load.wait()
        for f in pair:
            first_stage(f)
        if pair[0] == 0:
            for load in loads[3:]:
                load.wait()
        heat_y = left_stacked(down_u[...], q[...]) if pair[0] == 2 else None
        for f in pair:
            second_stage(f, heat_y)
        for stage in (across, defect, packet):
            for f in pair:
                stage(f)

    def pack(p, _):
        values = []
        for half in range(2):
            for f in range(4):
                values.append(g_s[f, pl.ds(half * 8 * CY + p, 8, stride=CY), :])
        for t, value in enumerate(chunk_transpose(values)):
            send_s[t * BLOCKS + p] = value
        return 0

    lax.fori_loop(0, BLOCKS, pack, 0, unroll=8)
    store(send_s, send_hbm, send_sem)
    for copy in stores:
        copy.wait()


def mode_kernel(g, lam_xy, lam_z, lanes, zf, zb, out):
    lam = lam_z[...] + lam_xy[...]
    nu, other, couple, product = (lanes[pl.ds(i, 1)] for i in range(4))
    own = nu * lam
    partner = other * lam
    half_square = 0.5 * SLAB_TIME * SLAB_TIME
    diagonal = 1.0 + SLAB_TIME * own + half_square * (own * own + product)
    mixing = couple * (SLAB_TIME + half_square * (own + partner))
    lane = lax.broadcasted_iota(jnp.int32, (CZ, 128), 1)
    even = (lane & CHUNK) == 0
    left_half = lane < 64

    state = None
    states = [jnp.zeros((CZ, 128), F32)]
    for s in range(SLABS):
        both = left(zf, g[pl.ds(s * BLOCKS * 8, BLOCKS * 8)])
        source = both[:CZ] + rolled(both[CZ:], 64, 1)
        if state is None:
            state = source
        else:
            swapped = jnp.where(even, rolled(state, -CHUNK, 1), rolled(state, CHUNK, 1))
            state = diagonal * state + mixing * swapped + source
        state = jnp.where(left_half, state, 0.0)
        states.append(state)
    for s in range(SLABS):
        packed = states[s] + rolled(states[s + 1], 64, 1)
        out[pl.ds(s * CZ, CZ)] = left(zb, packed)


def paired(x, axis):
    index = lax.broadcasted_iota(jnp.int32, x.shape, axis)
    return x + jnp.where((index & 1) == 0, rolled(x, -1, axis), rolled(x, 1, axis))


def end_kernel(second_hbm, low_hbm, high_hbm, second_out, mean_out, second, low, high, end, mean_s, in_sem, out_sem):
    loads = []
    for f in range(4):
        far = pl.ds(2 * PLANE, 4 * PLANE)
        moves = ((second_hbm.at[f], second), (low_hbm.at[f, far], low), (high_hbm.at[f, far], high))
        for i, (source, target) in enumerate(moves):
            load = pltpu.make_async_copy(source, target.at[f], in_sem.at[f, i])
            load.start()
            loads.append(load)
    stores = []
    for f in range(4):
        for load in loads[3 * f:3 * f + 3]:
            load.wait()
        for k in range(COARSE):
            values = []
            for p in (2 * k, 2 * k + 1):
                value = second[f, pl.ds(p * PLANE, PLANE)]
                if p < 4:
                    value = value + low[f, pl.ds(p * PLANE, PLANE)]
                else:
                    value = value + high[f, pl.ds((p - 4) * PLANE, PLANE)]
                values.append(value)
            mean = paired(paired(0.125 * (values[0] + values[1]), 0), 1)
            mean_s[f, pl.ds(k * PLANE, PLANE)] = mean
            for i in range(2):
                end[f, pl.ds((2 * k + i) * PLANE, PLANE)] = values[i] - mean
        for i, (source, target) in enumerate(((end, second_out), (mean_s, mean_out))):
            store = pltpu.make_async_copy(source.at[f], target.at[f], out_sem.at[f, i])
            store.start()
            stores.append(store)
    for store in stores:
        store.wait()


def middle_kernel(flags, first_hbm, low_hbm, high_hbm, mean_hbm, u_hbm, out_hbm, first, low, high, mean, u, out, in_sem, out_sem):
    mu = flags[0]
    loads = []
    for f in range(4):
        near = pl.ds(0, 2 * PLANE)
        moves = ((first_hbm.at[f], first), (low_hbm.at[f, near], low), (high_hbm.at[f, near], high), (mean_hbm.at[f], mean), (u_hbm.at[0, f], u))
        for i, (source, target) in enumerate(moves):
            load = pltpu.make_async_copy(source, target.at[f], in_sem.at[f, i])
            load.start()
            loads.append(load)
    stores = []
    for f in range(4):
        for load in loads[5 * f:5 * f + 5]:
            load.wait()
        for k in range(COARSE):
            pair = [pl.ds((2 * k + i) * PLANE, PLANE) for i in range(2)]
            start = paired(paired((0.125 * mu) * (u[f, pair[0]] + u[f, pair[1]]), 0), 1)
            middle = 0.5 * (mean[f, pl.ds(k * PLANE, PLANE)] + start)
            for i, rows in enumerate(pair):
                p = 2 * k + i
                value = first[f, rows] - middle
                if p < 2:
                    value = value + low[f, pl.ds(p * PLANE, PLANE)]
                if p >= FINE - 2:
                    value = value + high[f, pl.ds((p - FINE + 2) * PLANE, PLANE)]
                out[f, rows] = value
        store = pltpu.make_async_copy(out.at[f], out_hbm.at[f], out_sem.at[f])
        store.start()
        stores.append(store)
    for store in stores:
        store.wait()


def doubled(x):
    return jnp.concatenate([x[(p // 2) * PLANE:(p // 2 + 1) * PLANE] for p in range(FINE)], axis=0)


def nodes_kernel(flags, modes, first_hbm, second_hbm, before_hbm, yb, xb, u_hbm, out, h_s, first, second, before, u, out_s, in_sem, sem):
    leading = 1.0 - flags[0]
    loads = []
    for f in range(4):
        moves = ((first_hbm.at[f], first), (second_hbm.at[f], second), (before_hbm.at[f], before), (u_hbm.at[0, f], u))
        for i, (source, target) in enumerate(moves):
            load = pltpu.make_async_copy(source, target.at[f], in_sem.at[f, i])
            load.start()
            loads.append(load)
    for r in range(8):
        values = [modes[pl.ds(t * 64 + r * 8, 8)] for t in range(SLABS)]
        for g, value in enumerate(chunk_transpose(values)):
            h_s[g, pl.ds(r * 8, 8)] = value
    stores = []
    for f in range(4):
        start = right(left(yb, h_s[f]), xb)
        end = right(left(yb, h_s[4 + f]), xb)
        for load in loads[4 * f:4 * f + 4]:
            load.wait()
        out_s[0, f] = before[f] + leading * u[f] + doubled(start)
        out_s[1, f] = first[f] + doubled(0.5 * (start + end))
        out_s[2, f] = second[f] + doubled(end)
        for n in range(3):
            store = pltpu.make_async_copy(out_s.at[n, f], out.at[n, f], sem.at[n, f])
            store.start()
            stores.append(store)
    for store in stores:
        store.wait()


VM = pl.BlockSpec(memory_space=pltpu.VMEM)
SM = pl.BlockSpec(memory_space=pltpu.SMEM)
ANY = pl.BlockSpec(memory_space=pl.ANY)


GRANT = 60
END_COST = 60
MODE_COST = 20
MIDDLE_COST = 5


def params(mib):
    return pltpu.CompilerParams(vmem_limit_bytes=mib << 20)


def cost(microseconds):
    return pl.CostEstimate(flops=int(microseconds * 1e9), bytes_accessed=0, transcendentals=0)


def shape(*sizes):
    return jax.ShapeDtypeStruct(sizes, F32)


def scratch(*sizes):
    return pltpu.VMEM(sizes, F32)


def like(constant):
    return pltpu.VMEM(constant.shape, constant.dtype)


def per_device(fine_nodes, heating):
    u = fine_nodes.reshape(3, 4, OWN, NX)
    heat = heating.reshape(OWN, NX)
    tm = lax.axis_index("tm")
    space = lax.axis_index("space")
    flags = jnp.stack([tm > 0, space > 0, space < BLOCKS - 1, space < 0]).astype(F32)
    field = (4, OWN, NX)
    spill = (4, 6 * PLANE, NX)
    near = (4, 2 * PLANE, NX)
    far = (4, 4 * PLANE, NX)
    half = (4, OWN // 2, NX)
    tables = (STEP1, STEP2, ALONG, DOWN_C, DOWN_S, DOWN_U, X0, X1, LAM_XY)
    up_pairs = [(i, i + 1) for i in range(BLOCKS - 1)]
    down_pairs = [(i + 1, i) for i in range(BLOCKS - 1)]
    dma = pltpu.SemaphoreType.DMA

    with jax.named_scope("fine"):
        first_c, second_c, up, down, packet = pl.pallas_call(
            fine_kernel,
            out_shape=[shape(*field), shape(*field), shape(*spill), shape(*spill),
                       shape(SLABS * BLOCKS, 8, 128)],
            in_specs=[SM] + [ANY] * (2 + len(tables)),
            out_specs=[ANY] * 5,
            scratch_shapes=[scratch(3, 4, OWN, NX), scratch(OWN, NX)] + [like(table) for table in tables] + [
                scratch(*field),
                scratch(4, 12 * PLANE, NX),
                scratch(4, 12 * PLANE, NX),
                scratch(4, 16 * PLANE, NX),
                scratch(4, 10 * CY, NX),
                scratch(4, 12 * CY, NX),
                scratch(4, 8 * CY, NX),
                scratch(4, 10 * CY, CX),
                scratch(4, 8 * CY, CX),
                scratch(4, 4 * CY, CX),
                scratch(4, 16 * CY, CX),
                scratch(SLABS * BLOCKS, 8, 128),
                dma((10,)), dma((3, 4)), dma((4, 6)), dma,
            ],
            compiler_params=params(GRANT),
        )(flags, u, heat, *tables)

    with jax.named_scope("to_modes"):
        modes = lax.all_to_all(packet, AXES, 0, 0, tiled=True)

    with jax.named_scope("spill"):
        low = lax.ppermute(up, "space", up_pairs)
        high = lax.ppermute(down, "space", down_pairs)

    with jax.named_scope("end"):
        second, mean = pl.pallas_call(
            end_kernel,
            out_shape=[shape(*field), shape(*half)],
            in_specs=[ANY] * 3,
            out_specs=[ANY] * 2,
            scratch_shapes=[scratch(*field), scratch(*far), scratch(*far), scratch(*field), scratch(*half), dma((4, 3)), dma((4, 2))],
            cost_estimate=cost(END_COST),
            compiler_params=params(GRANT),
        )(second_c, low, high)

    with jax.named_scope("pass"):
        before = lax.ppermute(second, "tm", [(i, i + 1) for i in range(SLABS - 1)])

    with jax.named_scope("modes"):
        lam_xy = lax.dynamic_slice(jnp.asarray(MODE_XY), (tm * BLOCKS + space, 0), (1, 128))
        solved = pl.pallas_call(
            mode_kernel,
            out_shape=shape(SLABS * CZ, 128),
            in_specs=[VM] * 6,
            out_specs=VM,
            cost_estimate=cost(MODE_COST),
            compiler_params=params(16),
        )(modes.reshape(SLABS * BLOCKS * 8, 128), lam_xy, LAM_Z_COLUMN, LANES, ZF, ZB)

    with jax.named_scope("middle"):
        first = pl.pallas_call(
            middle_kernel,
            out_shape=shape(*field),
            in_specs=[SM] + [ANY] * 5,
            out_specs=ANY,
            scratch_shapes=[scratch(*field), scratch(*near), scratch(*near), scratch(*half), scratch(*field), scratch(*field),
                            dma((4, 5)), dma((4,))],
            cost_estimate=cost(MIDDLE_COST),
            compiler_params=params(GRANT),
        )(flags, first_c, low, high, mean, u)

    with jax.named_scope("from_modes"):
        solved = solved.reshape(SLABS * BLOCKS, COARSE, 128)
        back = lax.all_to_all(solved, AXES, 0, 0, tiled=True).reshape(SLABS * CZ, 128)

    with jax.named_scope("nodes"):
        out = pl.pallas_call(
            nodes_kernel,
            out_shape=shape(3, *field),
            in_specs=[SM, VM, ANY, ANY, ANY, VM, VM, ANY],
            out_specs=ANY,
            scratch_shapes=[scratch(8, 64, 128)] + [scratch(*field)] * 4 + [scratch(3, *field), dma((4, 4)), dma((3, 4))],
            cost_estimate=cost(5),
            compiler_params=params(GRANT),
        )(flags, back, first, second, before, YB, XB, u)
    return out.reshape(1, 3, 4, FINE, NY, NX)


def solution(mesh):
    in_specs = (P("tm", None, None, "space", None, None), P("space", None, None))
    out_specs = P("tm", None, None, "space", None, None)
    return jax.shard_map(
        per_device, mesh=mesh, in_specs=in_specs, out_specs=out_specs, check_vma=False
    )
```

```python
import numpy as np
import jax
import jax.numpy as jnp
from jax import lax
from jax.experimental import pallas as pl
from jax.experimental.pallas import tpu as pltpu
from jax.sharding import PartitionSpec as P

VISCOSITY = 0.4
DIFFUSIVITY = 0.3
SLAB_TIME = 0.25
HALF_TIME = 0.125

SLABS = 8
BLOCKS = 16
NZ, NY, NX = 128, 32, 256
CZ, CY, CX = NZ // 2, NY // 2, NX // 2
FINE = NZ // BLOCKS
COARSE = CZ // BLOCKS
CHUNK = CX // SLABS
SPILL = 5
AXES = ("tm", "space")
F32 = jnp.float32
BF16 = jnp.bfloat16


def real_basis(count):
    j = np.arange(count)
    rows, values = [], []
    for k in range(count):
        theta = 2.0 * np.pi * k / count
        if k == 0:
            row = np.ones(count)
        elif 2 * k == count:
            row = np.cos(np.pi * j)
        elif 2 * k < count:
            row = np.cos(theta * j) * np.sqrt(2.0)
        else:
            row = np.sin(theta * j) * np.sqrt(2.0)
        rows.append(row / np.sqrt(count))
        values.append((32.0 * np.cos(theta) - 2.0 * np.cos(2.0 * theta) - 30.0) / 48.0)
    return np.array(rows), np.array(values)


def pairs(count):
    return np.repeat(np.eye(count), 2, axis=0)


def circulant(count):
    eye = np.eye(count)
    return (
        16.0 * (np.roll(eye, 1, 0) + np.roll(eye, -1, 0))
        - (np.roll(eye, 2, 0) + np.roll(eye, -2, 0))
        - 30.0 * eye
    )


def split(matrix):
    matrix = np.asarray(matrix, np.float32)
    high = matrix.astype(jnp.bfloat16)
    low = (matrix - high.astype(np.float32)).astype(jnp.bfloat16)
    return np.stack([high, low])


FY, LAM_Y = real_basis(CY)
FX, LAM_X = real_basis(CX)


def depth_basis():
    eye = np.eye(CZ)
    band = -30.0 * eye
    for offset, weight in ((1, 16.0), (2, -1.0)):
        band += weight * (np.eye(CZ, k=offset) + np.eye(CZ, k=-offset))
    values, vectors = np.linalg.eigh(band / 48.0)
    return values, vectors


LAM_Z, QZ = depth_basis()

DOWN_X = (FX @ pairs(CX).T * 0.5).T
DOWN_XL = circulant(NX) @ DOWN_X
UP_Y = pairs(CY) @ FY.T
UP_X = FX @ pairs(CX).T


def exact(matrix):
    high = np.asarray(matrix, np.float32).astype(jnp.bfloat16)
    assert np.array_equal(high.astype(np.float64), matrix)
    return high


def stacked(matrix):
    return split(matrix).reshape(-1, matrix.shape[1])


ALONG = exact(circulant(NX))
PLANES = 11
F11 = stacked(np.kron(np.eye(PLANES), FY))
X0 = split(DOWN_X)
X1 = split(DOWN_XL)
LAM_XY = (LAM_Y[:, None] + LAM_X[None, :]).astype(np.float32)


def depth_forward():
    table = np.zeros((2, CZ, BLOCKS, 8))
    for half in range(2):
        for block in range(BLOCKS):
            for slot in range(8):
                z = block * COARSE + half * 8 + slot - SPILL
                if 0 <= z < CZ:
                    table[half, :, block, slot] = QZ[z]
    return table.reshape(2 * CZ, BLOCKS * 8)


ZF = split(depth_forward())
ZB = split(QZ)


def up_y_table():
    table = np.zeros((COARSE, NY, CY, COARSE))
    for z in range(COARSE):
        table[z, :, :, z] = UP_Y
    return table.reshape(COARSE * NY, CY * COARSE)


YB = split(up_y_table())
XB = split(UP_X)


def mode_values():
    table = np.zeros((SLABS, BLOCKS, 2, 4, CHUNK))
    for t in range(SLABS):
        for p in range(BLOCKS):
            table[t, p] = LAM_Y[p] + LAM_X[t * CHUNK:(t + 1) * CHUNK]
    return table.reshape(SLABS * BLOCKS, 128).astype(np.float32)


def lane_constants():
    own = np.array([VISCOSITY, VISCOSITY, VISCOSITY, DIFFUSIVITY])
    partner = np.array([VISCOSITY, VISCOSITY, DIFFUSIVITY, VISCOSITY])
    couple = np.array([2.0, -2.0, 1.0, 1.0])
    product = np.array([-4.0, -4.0, 1.0, 1.0])
    table = np.zeros((8, 2, 4, CHUNK))
    for row, values in enumerate((own, partner, couple, product)):
        table[row] = values[None, :, None]
    return table.reshape(8, 128).astype(np.float32)


MODE_XY = mode_values()
LANES = lane_constants()
LAM_Z_COLUMN = np.repeat(LAM_Z[:, None], 128, axis=1).astype(np.float32)


def halves(x):
    high = x.astype(BF16)
    return high, (x - high.astype(F32)).astype(BF16)


def dot(a, b):
    return jnp.dot(a, b, preferred_element_type=F32)


def left(table, x):
    high, low = halves(x)
    return dot(table[0], high) + (dot(table[0], low) + dot(table[1], high))


def right(x, table):
    high, low = halves(x)
    return dot(high, table[0]) + (dot(low, table[0]) + dot(high, table[1]))


def rolled(x, by, axis):
    return pltpu.roll(x, by % x.shape[axis], axis)


def across_y(x):
    near = rolled(x, 1, 0) + rolled(x, -1, 0)
    far = rolled(x, 2, 0) + rolled(x, -2, 0)
    return 16.0 * near - far


def total(terms):
    out = terms[0]
    for term in terms[1:]:
        out = out + term
    return out


def chunk_transpose(values):
    values = list(values)
    lane = lax.broadcasted_iota(jnp.int32, values[0].shape, 1)
    for bit in (1, 2, 4):
        shift = CHUNK * bit
        low = (lane & shift) == 0
        for i in range(8):
            if i & bit:
                continue
            j = i | bit
            first, second = values[i], values[j]
            values[i] = jnp.where(low, first, rolled(second, shift, 1))
            values[j] = jnp.where(low, rolled(first, -shift, 1), second)
    return values


def left_stacked(table, x):
    high, low = halves(x)
    rows = table.shape[0] // 2
    both = dot(table, high)
    return both[:rows] + (both[rows:] + dot(table[:rows], low))


PLANE = NY
OWN = FINE * PLANE


def position():
    tm, space = lax.axis_index("tm"), lax.axis_index("space")
    one = jnp.float32(1.0)
    zero = jnp.float32(0.0)
    return jnp.where(tm > 0, one, zero), jnp.where(space > 0, one, zero), jnp.where(space < BLOCKS - 1, one, zero)


def fine_kernel(u_hbm, q_hbm, along_hbm, f11_hbm, x0_hbm, x1_hbm, lam_hbm,
                first_hbm, second_hbm, up_hbm, down_hbm, send_hbm,
                u, q, along, f11, x0, x1, lam,
                a_s, fe, be, se, cs, rows_s, pair_s, y_s, w_s, g_s, send_s, in_sem, u_sem, out_sem, send_sem):
    mu, keep_low, keep_high = position()
    loads = [
        pltpu.make_async_copy(source, target, in_sem.at[i])
        for i, (source, target) in enumerate((
            (along_hbm, along), (x0_hbm, x0), (x1_hbm, x1), (f11_hbm, f11), (lam_hbm, lam), (q_hbm, q)))
    ]
    node_loads = [
        [pltpu.make_async_copy(u_hbm.at[n, f], u.at[n, f], u_sem.at[n, f]) for n in range(3)] for f in range(4)
    ]
    for load in node_loads[0] + loads[:1] + node_loads[1] + loads[1:5] + node_loads[2] + node_loads[3] + loads[5:]:
        load.start()

    edge = 2 * PLANE
    middle = pl.ds(edge, OWN)
    stores = []

    def store(source, target, sem):
        copy = pltpu.make_async_copy(source, target, sem)
        copy.start()
        stores.append(copy)

    def field(f):
        nu = DIFFUSIVITY if f == 3 else VISCOSITY
        return nu, (2.0, -2.0, 1.0, 1.0)[f], f ^ 1

    def fine_plane(ref, f, p, low):
        return ref[f, pl.ds((p - low) * PLANE, PLANE)]

    def depth(ref, f, p, low, high):
        near = [fine_plane(ref, f, p + o, low) for o in (-1, 1) if low <= p + o < high]
        far = [fine_plane(ref, f, p + o, low) for o in (-2, 2) if low <= p + o < high]
        if not near:
            return -total(far)
        return 16.0 * total(near) - total(far) if far else 16.0 * total(near)

    def along_x(x):
        high, low = halves(x)
        return dot(high, along[...]) + dot(low, along[...])

    def combine(f):
        for load in node_loads[f]:
            load.wait()
        a_s[f] = (5.0 / 24.0) * u[0, f] + (1.0 / 3.0) * u[1, f] - (1.0 / 24.0) * u[2, f]

    def first_stage(f):
        nu, couple, partner = field(f)
        scale = nu * (SLAB_TIME / 12.0)
        row = along_x(a_s[f])
        for p in range(-2, FINE + 2):
            here = pl.ds((p + 2) * PLANE, PLANE)
            acc = depth(a_s, f, p, 0, FINE)
            if 0 <= p < FINE:
                own = pl.ds(p * PLANE, PLANE)
                centre = a_s[f, own]
                start = u[0, f, own]
                acc = acc + (across_y(centre) - 60.0 * centre) + row[p * PLANE:(p + 1) * PLANE]
                value = scale * acc + (couple * SLAB_TIME) * a_s[partner, own] + start
                if f == 3:
                    value = value + HALF_TIME * q[own]
                be[f, here] = 0.5 * value + ((-1.0 / 24.0) * start - (1.0 / 6.0) * u[1, f, own] + (5.0 / 24.0) * u[2, f, own])
            else:
                value = (scale * (keep_low if p < 0 else keep_high)) * acc
                be[f, here] = 0.5 * value
            fe[f, here] = value
        store(fe.at[f, middle], first_hbm.at[f], out_sem.at[f, 0])
        store(fe.at[f, pl.ds(0, edge)], down_hbm.at[f, pl.ds(0, edge)], out_sem.at[f, 1])
        store(fe.at[f, pl.ds(edge + OWN, edge)], up_hbm.at[f, pl.ds(0, edge)], out_sem.at[f, 2])

    def second_stage(f):
        nu, couple, partner = field(f)
        scale = nu * (SLAB_TIME / 12.0)
        row = along_x(be[f])
        for p in range(-4, FINE + 4):
            here = pl.ds((p + 4) * PLANE, PLANE)
            acc = depth(be, f, p, -2, FINE + 2)
            mask = keep_low if p < 0 else keep_high
            if -2 <= p < FINE + 2:
                inner = pl.ds((p + 2) * PLANE, PLANE)
                centre = be[f, inner]
                first = fe[f, inner]
                acc = acc + (across_y(centre) - 60.0 * centre) + row[(p + 2) * PLANE:(p + 3) * PLANE]
                value = scale * acc + (couple * SLAB_TIME) * be[partner, inner] + first
                if 0 <= p < FINE:
                    own = pl.ds(p * PLANE, PLANE)
                    if f == 3:
                        value = value + HALF_TIME * q[own]
                    c = (1.0 / 6.0) * (value + u[0, f, own]) + (2.0 / 3.0) * first
                else:
                    value = mask * value
                    c = (1.0 / 6.0) * value + (2.0 / 3.0) * first
            else:
                value = (scale * mask) * acc
                c = (1.0 / 6.0) * value
            se[f, here] = value
            cs[f, here] = c
        store(se.at[f, pl.ds(2 * edge, OWN)], second_hbm.at[f], out_sem.at[f, 3])
        store(se.at[f, pl.ds(0, 2 * edge)], down_hbm.at[f, pl.ds(edge, 2 * edge)], out_sem.at[f, 4])
        store(se.at[f, pl.ds(2 * edge + OWN, 2 * edge)], up_hbm.at[f, pl.ds(edge, 2 * edge)], out_sem.at[f, 5])

    def put(ref, f, k, value):
        for i in range(2):
            ref[f, i, pl.ds(k * PLANE, PLANE)] = value[:, i * 128:(i + 1) * 128]

    def every_other(ref, f, start, count):
        return jnp.concatenate([ref[f, i, pl.ds(start, count, stride=2), :] for i in range(2)], axis=1)

    def coarse_means(f):
        nu, couple, partner = field(f)
        scale = nu * (SLAB_TIME / 12.0)

        def pair_sum(ref, g, k):
            return fine_plane(ref, g, 2 * k, -4) + fine_plane(ref, g, 2 * k + 1, -4)

        for k in range(-3, COARSE + 3):
            value = None
            inside = -2 <= k < COARSE + 2
            if inside:
                mean = pair_sum(cs, f, k)
                put(pair_s, f, k + 2, mean)
                value = (-7.0 * scale) * mean + (couple * (SLAB_TIME * 0.5)) * pair_sum(cs, partner, k)
            for weight, planes in ((7.5, (2 * k - 1, 2 * k + 2)), (-0.5, (2 * k - 2, 2 * k + 3))):
                part = [fine_plane(cs, f, p, -4) for p in planes if -4 <= p < FINE + 4]
                if part:
                    part = (weight * scale) * total(part)
                    value = part if value is None else value + part
            if f == 3 and 0 <= k < COARSE:
                value = value + (0.5 * SLAB_TIME) * (q[pl.ds(2 * k * PLANE, PLANE)] + q[pl.ds((2 * k + 1) * PLANE, PLANE)])
            if k < 0:
                value = keep_low * value
            if k >= COARSE:
                value = keep_high * value
            if inside:
                last = 0.5 * pair_sum(se, f, k)
                value = value - last
                if 0 <= k < COARSE:
                    start = 0.5 * (u[0, f, pl.ds(2 * k * PLANE, PLANE)] + u[0, f, pl.ds((2 * k + 1) * PLANE, PLANE)])
                    value = value + start
                    last = last - mu * start
                    put(rows_s, f, 18 + k, start)
                put(rows_s, f, 12 + k, last)
            put(rows_s, f, k + 3, value)

    def across(f):
        nu, _, _ = field(f)
        scale = nu * (SLAB_TIME / 12.0)
        count = 22 * CY
        y = 0.5 * (every_other(rows_s, f, 0, count) + every_other(rows_s, f, 1, count))
        even = every_other(pair_s, f, 0, 8 * CY)
        odd = every_other(pair_s, f, 1, 8 * CY)
        mean = even + odd
        curved = []
        for k in range(8):
            rows = slice(k * CY, (k + 1) * CY)
            e, o = even[rows], odd[rows]
            near = rolled(o, 1, 0) + rolled(e, -1, 0)
            far = rolled(e, 1, 0) + rolled(o, -1, 0)
            value = (0.25 * scale) * (15.0 * near - far - 14.0 * mean[rows])
            if k < 2:
                value = keep_low * value
            if k >= 6:
                value = keep_high * value
            curved.append(value)
        y = jnp.concatenate([y[:CY], y[CY:9 * CY] + jnp.concatenate(curved, axis=0), y[9 * CY:]], axis=0)
        both = right(y, x0)
        bent = (0.25 * scale) * right(mean, x1)
        return jnp.concatenate([both[:CY], both[CY:9 * CY] + bent, both[9 * CY:]], axis=0)

    def to_y_modes(pair):
        both = jnp.concatenate([across(f) for f in pair], axis=1)
        half = PLANES * CY
        out = [left_stacked(f11[...], both[i * half:(i + 1) * half]) for i in range(2)]
        out = jnp.concatenate(out, axis=0)
        for i, f in enumerate(pair):
            lanes = slice(i * CX, (i + 1) * CX)
            w_s[f] = out[:18 * CY, lanes]
            y_s[f] = out[18 * CY:, lanes]

    def kept(value, p, count):
        if p < 0:
            return value * keep_low
        if p >= count:
            return value * keep_high
        return value

    def plane(ref, f, k, low, high):
        if low <= k < high:
            return ref[f, pl.ds((k - low) * CY, CY)]
        return None

    def node_plane(f, k):
        if -2 <= k < COARSE + 2:
            return w_s[f, pl.ds((12 + k) * CY, CY)]
        return None

    def coarse_slope(ref, f, k, low, high):
        nu, couple, partner = field(f)
        out = None
        for weight, offsets in ((16.0 / 48.0, (-1, 1)), (-1.0 / 48.0, (-2, 2))):
            part = [plane(ref, f, k + o, low, high) for o in offsets]
            part = [value for value in part if value is not None]
            if part:
                part = weight * total(part)
                out = part if out is None else out + part
        centre = plane(ref, f, k, low, high)
        if centre is None:
            return nu * out
        out = out + (lam[...] - 30.0 / 48.0) * centre
        return nu * out + couple * plane(ref, partner, k, low, high)

    def defect(f):
        for k in range(-2, COARSE + 2):
            value = coarse_slope(y_s, f, k, 0, COARSE)
            value = kept((mu * SLAB_TIME) * value, k, COARSE)
            rows = pl.ds((k + 3) * CY, CY)
            w_s[f, rows] = w_s[f, rows] - value

    def packet(f):
        for k in range(-SPILL, 16 - SPILL):
            rows = pl.ds((k + SPILL) * CY, CY)
            if k >= COARSE + SPILL:
                g_s[f, rows] = jnp.zeros((CY, CX), F32)
                continue
            value = kept(HALF_TIME * coarse_slope(w_s, f, k, -3, COARSE + 3), k, COARSE)
            for part in (plane(w_s, f, k, -3, COARSE + 3), node_plane(f, k)):
                if part is not None:
                    value = value + part
            g_s[f, rows] = value

    for pair in ((0, 1), (2, 3)):
        for f in pair:
            combine(f)
        if pair[0] == 0:
            loads[0].wait()
        else:
            loads[5].wait()
        for f in pair:
            first_stage(f)
        for f in pair:
            second_stage(f)
        for f in pair:
            coarse_means(f)
        if pair[0] == 0:
            for load in loads[1:5]:
                load.wait()
        to_y_modes(pair)
        for stage in (defect, packet):
            for f in pair:
                stage(f)

    def pack(p, _):
        values = []
        for half in range(2):
            for f in range(4):
                values.append(g_s[f, pl.ds(half * 8 * CY + p, 8, stride=CY), :])
        for t, value in enumerate(chunk_transpose(values)):
            send_s[t * BLOCKS + p] = value
        return 0

    lax.fori_loop(0, BLOCKS, pack, 0, unroll=8)
    store(send_s, send_hbm, send_sem)
    for copy in stores:
        copy.wait()


def mode_kernel(g, xy, lam_z, lanes, zf, zb, out):
    index = lax.axis_index("tm") * BLOCKS + lax.axis_index("space")
    lam = lam_z[...] + xy[pl.ds(index, 1)]
    nu, other, couple, product = (lanes[pl.ds(i, 1)] for i in range(4))
    own = nu * lam
    partner = other * lam
    half_square = 0.5 * SLAB_TIME * SLAB_TIME
    diagonal = 1.0 + SLAB_TIME * own + half_square * (own * own + product)
    mixing = couple * (SLAB_TIME + half_square * (own + partner))
    lane = lax.broadcasted_iota(jnp.int32, (CZ, 128), 1)
    even = (lane & CHUNK) == 0
    left_half = lane < 64

    state = None
    states = [jnp.zeros((CZ, 128), F32)]
    for s in range(SLABS):
        both = left(zf, g[pl.ds(s * BLOCKS * 8, BLOCKS * 8)])
        source = both[:CZ] + rolled(both[CZ:], 64, 1)
        if state is None:
            state = source
        else:
            swapped = jnp.where(even, rolled(state, -CHUNK, 1), rolled(state, CHUNK, 1))
            state = diagonal * state + mixing * swapped + source
        state = jnp.where(left_half, state, 0.0)
        states.append(state)
    for s in range(SLABS):
        packed = states[s] + rolled(states[s + 1], 64, 1)
        out[pl.ds(s * CZ, CZ)] = left(zb, packed)


def paired(x, axis):
    index = lax.broadcasted_iota(jnp.int32, x.shape, axis)
    return x + jnp.where((index & 1) == 0, rolled(x, -1, axis), rolled(x, 1, axis))


def block_mean(x, weight):
    return paired(paired(weight * x, 0), 1)


def middle_kernel(first_hbm, low_hbm, high_hbm, most_hbm, rest_hbm, u_hbm, first_out, second_out,
                  first, low, high, second, u, out, in_sem, out_sem):
    mu, _, _ = position()
    near = pl.ds(0, 2 * PLANE)
    loads = []
    for f in range(4):
        source = most_hbm.at[f] if f < SENT_FIRST else rest_hbm.at[f - SENT_FIRST]
        moves = ((first_hbm.at[f], first), (low_hbm.at[f, near], low), (high_hbm.at[f, near], high), (source, second), (u_hbm.at[0, f], u))
        for i, (source, target) in enumerate(moves):
            load = pltpu.make_async_copy(source, target.at[f], in_sem.at[f, i])
            load.start()
            loads.append(load)
    stores = []
    for f in range(4):
        for load in loads[5 * f:5 * f + 5]:
            load.wait()
        for k in range(COARSE):
            pair = [pl.ds((2 * k + i) * PLANE, PLANE) for i in range(2)]
            seconds = [second[f, rows] for rows in pair]
            mean = block_mean(seconds[0] + seconds[1], 0.125)
            start = block_mean(u[f, pair[0]] + u[f, pair[1]], 0.125 * mu)
            middle = 0.5 * (mean + start)
            for i, rows in enumerate(pair):
                p = 2 * k + i
                value = first[f, rows] - middle
                if p < 2:
                    value = value + low[f, pl.ds(p * PLANE, PLANE)]
                if p >= FINE - 2:
                    value = value + high[f, pl.ds((p - FINE + 2) * PLANE, PLANE)]
                out[0, f, rows] = value
                out[1, f, rows] = seconds[i] - mean
        for n, target in enumerate((first_out, second_out)):
            store = pltpu.make_async_copy(out.at[n, f], target.at[f], out_sem.at[n, f])
            store.start()
            stores.append(store)
    for store in stores:
        store.wait()


def doubled(x):
    return jnp.concatenate([x[(p // 2) * PLANE:(p // 2 + 1) * PLANE] for p in range(FINE)], axis=0)


def nodes_kernel(modes, first_hbm, second_hbm, most_hbm, rest_hbm, yb_hbm, xb_hbm, u_hbm, out, h_s, first, second, before, yb, xb, out_s, in_sem, sem):
    mu, _, _ = position()
    leading = lax.axis_index("tm") == 0
    tables = [pltpu.make_async_copy(yb_hbm, yb, in_sem.at[0, 3]), pltpu.make_async_copy(xb_hbm, xb, in_sem.at[1, 3])]
    for load in tables:
        load.start()
    for f in range(4):
        for i, (source, target) in enumerate(((first_hbm, first), (second_hbm, second))):
            pltpu.make_async_copy(source.at[f], target.at[f], in_sem.at[f, i]).start()

        @pl.when(leading)
        def _():
            pltpu.make_async_copy(u_hbm.at[0, f], before.at[f], in_sem.at[f, 2]).start()

        @pl.when(jnp.logical_not(leading))
        def _():
            source = most_hbm.at[f] if f < SENT_FIRST else rest_hbm.at[f - SENT_FIRST]
            pltpu.make_async_copy(source, before.at[f], in_sem.at[f, 2]).start()

    for r in range(8):
        values = [modes[pl.ds(t * 64 + r * 8, 8)] for t in range(SLABS)]
        for g, value in enumerate(chunk_transpose(values)):
            h_s[g, pl.ds(r * 8, 8)] = value
    for load in tables:
        load.wait()
    stores = []
    for f in range(4):
        start = right(left(yb, h_s[f]), xb)
        end = right(left(yb, h_s[4 + f]), xb)
        for i, (source, target) in enumerate(((first_hbm, first), (second_hbm, second), (second_hbm, before))):
            pltpu.make_async_copy(source.at[f], target.at[f], in_sem.at[f, i]).wait()
        for k in range(COARSE):
            pair = [pl.ds((2 * k + i) * PLANE, PLANE) for i in range(2)]
            value = [before[f, rows] for rows in pair]
            shift = start[k * PLANE:(k + 1) * PLANE] - block_mean(value[0] + value[1], 0.125 * mu)
            for i, rows in enumerate(pair):
                out_s[0, f, rows] = value[i] + shift
        out_s[1, f] = first[f] + doubled(0.5 * (start + end))
        out_s[2, f] = second[f] + doubled(end)
        for n in range(3):
            store = pltpu.make_async_copy(out_s.at[n, f], out.at[n, f], sem.at[n, f])
            store.start()
            stores.append(store)
    for store in stores:
        store.wait()


VM = pl.BlockSpec(memory_space=pltpu.VMEM)
ANY = pl.BlockSpec(memory_space=pl.ANY)


GRANT = 60
SENT_FIRST = 3
MODE_COST = 20
MIDDLE_COST = 5


def params(mib):
    return pltpu.CompilerParams(vmem_limit_bytes=mib << 20)


def cost(microseconds):
    return pl.CostEstimate(flops=int(microseconds * 1e9), bytes_accessed=0, transcendentals=0)


def shape(*sizes):
    return jax.ShapeDtypeStruct(sizes, F32)


def scratch(*sizes):
    return pltpu.VMEM(sizes, F32)


def like(constant):
    return pltpu.VMEM(constant.shape, constant.dtype)


def per_device(fine_nodes, heating):
    u = fine_nodes.reshape(3, 4, OWN, NX)
    heat = heating.reshape(OWN, NX)
    field = (4, OWN, NX)
    spill = (4, 6 * PLANE, NX)
    near = (4, 2 * PLANE, NX)
    tables = (ALONG, F11, X0, X1, LAM_XY)
    up_pairs = [(i, i + 1) for i in range(BLOCKS - 1)]
    down_pairs = [(i + 1, i) for i in range(BLOCKS - 1)]
    dma = pltpu.SemaphoreType.DMA

    with jax.named_scope("fine"):
        first_c, second_c, up, down, packet = pl.pallas_call(
            fine_kernel,
            out_shape=[shape(*field), shape(*field), shape(*spill), shape(*spill),
                       shape(SLABS * BLOCKS, 8, 128)],
            in_specs=[ANY] * (2 + len(tables)),
            out_specs=[ANY] * 5,
            scratch_shapes=[scratch(3, 4, OWN, NX), scratch(OWN, NX)] + [like(table) for table in tables] + [
                scratch(*field),
                scratch(4, 12 * PLANE, NX),
                scratch(4, 12 * PLANE, NX),
                scratch(4, 16 * PLANE, NX),
                scratch(4, 16 * PLANE, NX),
                scratch(4, 2, 22 * PLANE, 128),
                scratch(4, 2, 8 * PLANE, 128),
                scratch(4, 4 * CY, CX),
                scratch(4, 18 * CY, CX),
                scratch(4, 16 * CY, CX),
                scratch(SLABS * BLOCKS, 8, 128),
                dma((6,)), dma((3, 4)), dma((4, 6)), dma,
            ],
            compiler_params=params(GRANT),
        )(u, heat, *tables)

    with jax.named_scope("to_modes"):
        modes = lax.all_to_all(packet, AXES, 0, 0, tiled=True)

    with jax.named_scope("spill"):
        low = lax.ppermute(up, "space", up_pairs)
        high = lax.ppermute(down, "space", down_pairs)

    with jax.named_scope("end"):
        far = slice(2 * PLANE, 6 * PLANE)

        def ended(fields):
            return second_c[fields] + jnp.concatenate([low[fields, far], high[fields, far]], axis=1)

        most = ended(slice(0, SENT_FIRST))
        rest = ended(slice(SENT_FIRST, 4))

    with jax.named_scope("pass"):
        later = [(i, i + 1) for i in range(SLABS - 1)]
        most_before = lax.ppermute(most, "tm", later)

    with jax.named_scope("modes"):
        constants = (MODE_XY, LAM_Z_COLUMN, LANES, ZF, ZB)
        solved = pl.pallas_call(
            mode_kernel,
            out_shape=shape(SLABS * CZ, 128),
            in_specs=[VM] * 6,
            out_specs=VM,
            cost_estimate=cost(MODE_COST),
            compiler_params=params(16),
        )(modes.reshape(SLABS * BLOCKS * 8, 128), *constants)

    with jax.named_scope("pass_rest"):
        rest_sent, _ = lax.optimization_barrier((rest, solved))
        rest_before = lax.ppermute(rest_sent, "tm", later)

    with jax.named_scope("middle"):
        first, second = pl.pallas_call(
            middle_kernel,
            out_shape=[shape(*field)] * 2,
            in_specs=[ANY] * 6,
            out_specs=[ANY] * 2,
            scratch_shapes=[scratch(*field), scratch(*near), scratch(*near), scratch(*field), scratch(*field), scratch(2, *field),
                            dma((4, 5)), dma((2, 4))],
            cost_estimate=cost(MIDDLE_COST),
            compiler_params=params(GRANT),
        )(first_c, low, high, most, rest, u)

    with jax.named_scope("from_modes"):
        solved = solved.reshape(SLABS * BLOCKS, COARSE, 128)
        back = lax.all_to_all(solved, AXES, 0, 0, tiled=True).reshape(SLABS * CZ, 128)

    with jax.named_scope("nodes"):
        out = pl.pallas_call(
            nodes_kernel,
            out_shape=shape(3, *field),
            in_specs=[VM] + [ANY] * 7,
            out_specs=ANY,
            scratch_shapes=[scratch(8, 64, 128)] + [scratch(*field)] * 3 + [like(YB), like(XB), scratch(3, *field), dma((4, 4)), dma((3, 4))],
            cost_estimate=cost(5),
            compiler_params=params(GRANT),
        )(back, first, second, most_before, rest_before, YB, XB, u)
    return out.reshape(1, 3, 4, FINE, NY, NX)


def solution(mesh):
    in_specs = (P("tm", None, None, "space", None, None), P("space", None, None))
    out_specs = P("tm", None, None, "space", None, None)
    return jax.shard_map(
        per_device, mesh=mesh, in_specs=in_specs, out_specs=out_specs, check_vma=False
    )
```

```python
import numpy as np
import jax
import jax.numpy as jnp
from jax import lax
from jax.experimental import pallas as pl
from jax.experimental.pallas import tpu as pltpu
from jax.sharding import PartitionSpec as P

VISCOSITY = 0.4
DIFFUSIVITY = 0.3
SLAB_TIME = 0.25
HALF_TIME = 0.125

SLABS = 8
BLOCKS = 16
NZ, NY, NX = 128, 32, 256
CZ, CY, CX = NZ // 2, NY // 2, NX // 2
FINE = NZ // BLOCKS
COARSE = CZ // BLOCKS
CHUNK = CX // SLABS
SPILL = 5
AXES = ("tm", "space")
F32 = jnp.float32
BF16 = jnp.bfloat16


def real_basis(count):
    j = np.arange(count)
    rows, values = [], []
    for k in range(count):
        theta = 2.0 * np.pi * k / count
        if k == 0:
            row = np.ones(count)
        elif 2 * k == count:
            row = np.cos(np.pi * j)
        elif 2 * k < count:
            row = np.cos(theta * j) * np.sqrt(2.0)
        else:
            row = np.sin(theta * j) * np.sqrt(2.0)
        rows.append(row / np.sqrt(count))
        values.append((32.0 * np.cos(theta) - 2.0 * np.cos(2.0 * theta) - 30.0) / 48.0)
    return np.array(rows), np.array(values)


def pairs(count):
    return np.repeat(np.eye(count), 2, axis=0)


def circulant(count):
    eye = np.eye(count)
    return (
        16.0 * (np.roll(eye, 1, 0) + np.roll(eye, -1, 0))
        - (np.roll(eye, 2, 0) + np.roll(eye, -2, 0))
        - 30.0 * eye
    )


def split(matrix):
    matrix = np.asarray(matrix, np.float32)
    high = matrix.astype(jnp.bfloat16)
    low = (matrix - high.astype(np.float32)).astype(jnp.bfloat16)
    return np.stack([high, low])


FY, LAM_Y = real_basis(CY)
FX, LAM_X = real_basis(CX)


def depth_basis():
    eye = np.eye(CZ)
    band = -30.0 * eye
    for offset, weight in ((1, 16.0), (2, -1.0)):
        band += weight * (np.eye(CZ, k=offset) + np.eye(CZ, k=-offset))
    values, vectors = np.linalg.eigh(band / 48.0)
    return values, vectors


LAM_Z, QZ = depth_basis()

DOWN_X = (FX @ pairs(CX).T * 0.5).T
DOWN_XL = circulant(NX) @ DOWN_X
UP_Y = pairs(CY) @ FY.T
UP_X = FX @ pairs(CX).T


def exact(matrix):
    high = np.asarray(matrix, np.float32).astype(jnp.bfloat16)
    assert np.array_equal(high.astype(np.float64), matrix)
    return high


def stacked(matrix):
    return split(matrix).reshape(-1, matrix.shape[1])


ALONG = exact(circulant(NX))
PLANES = 11
F11 = stacked(np.kron(np.eye(PLANES), FY))
X0 = split(DOWN_X)
X1 = split(DOWN_XL)
LAM_XY = (LAM_Y[:, None] + LAM_X[None, :]).astype(np.float32)


def depth_forward():
    table = np.zeros((2, CZ, BLOCKS, 8))
    for half in range(2):
        for block in range(BLOCKS):
            for slot in range(8):
                z = block * COARSE + half * 8 + slot - SPILL
                if 0 <= z < CZ:
                    table[half, :, block, slot] = QZ[z]
    return table.reshape(2 * CZ, BLOCKS * 8)


ZF = split(depth_forward())
ZB = split(QZ)


def up_y_table():
    table = np.zeros((COARSE, NY, CY, COARSE))
    for z in range(COARSE):
        table[z, :, :, z] = UP_Y
    return table.reshape(COARSE * NY, CY * COARSE)


YB = split(up_y_table())
XB = split(UP_X)


def mode_values():
    table = np.zeros((SLABS, BLOCKS, 2, 4, CHUNK))
    for t in range(SLABS):
        for p in range(BLOCKS):
            table[t, p] = LAM_Y[p] + LAM_X[t * CHUNK:(t + 1) * CHUNK]
    return table.reshape(SLABS * BLOCKS, 128).astype(np.float32)


def lane_constants():
    own = np.array([VISCOSITY, VISCOSITY, VISCOSITY, DIFFUSIVITY])
    partner = np.array([VISCOSITY, VISCOSITY, DIFFUSIVITY, VISCOSITY])
    couple = np.array([2.0, -2.0, 1.0, 1.0])
    product = np.array([-4.0, -4.0, 1.0, 1.0])
    table = np.zeros((8, 2, 4, CHUNK))
    for row, values in enumerate((own, partner, couple, product)):
        table[row] = values[None, :, None]
    return table.reshape(8, 128).astype(np.float32)


MODE_XY = mode_values()
LANES = lane_constants()
LAM_Z_COLUMN = np.repeat(LAM_Z[:, None], 128, axis=1).astype(np.float32)


def halves(x):
    high = x.astype(BF16)
    return high, (x - high.astype(F32)).astype(BF16)


def dot(a, b):
    return jnp.dot(a, b, preferred_element_type=F32)


def left(table, x):
    high, low = halves(x)
    return dot(table[0], high) + (dot(table[0], low) + dot(table[1], high))


def right(x, table):
    high, low = halves(x)
    return dot(high, table[0]) + (dot(low, table[0]) + dot(high, table[1]))


def rolled(x, by, axis):
    return pltpu.roll(x, by % x.shape[axis], axis)


def across_y(x):
    near = rolled(x, 1, 0) + rolled(x, -1, 0)
    far = rolled(x, 2, 0) + rolled(x, -2, 0)
    return 16.0 * near - far


def total(terms):
    out = terms[0]
    for term in terms[1:]:
        out = out + term
    return out


def chunk_transpose(values):
    values = list(values)
    lane = lax.broadcasted_iota(jnp.int32, values[0].shape, 1)
    for bit in (1, 2, 4):
        shift = CHUNK * bit
        low = (lane & shift) == 0
        for i in range(8):
            if i & bit:
                continue
            j = i | bit
            first, second = values[i], values[j]
            values[i] = jnp.where(low, first, rolled(second, shift, 1))
            values[j] = jnp.where(low, rolled(first, -shift, 1), second)
    return values


def left_stacked(table, x):
    high, low = halves(x)
    rows = table.shape[0] // 2
    both = dot(table, high)
    return both[:rows] + (both[rows:] + dot(table[:rows], low))


PLANE = NY
OWN = FINE * PLANE


def position():
    tm, space = lax.axis_index("tm"), lax.axis_index("space")
    one = jnp.float32(1.0)
    zero = jnp.float32(0.0)
    return jnp.where(tm > 0, one, zero), jnp.where(space > 0, one, zero), jnp.where(space < BLOCKS - 1, one, zero)


def fine_kernel(u_hbm, q_hbm, along_hbm, f11_hbm, x0_hbm, x1_hbm, lam_hbm,
                first_hbm, second_hbm, near_hbm, across_hbm, send_hbm,
                u, q, along, f11, x0, x1, lam,
                a_s, fe, be, se, cs, rows_s, pair_s, y_s, w_s, g_s, send_s, in_sem, u_sem, out_sem, send_sem):
    mu, keep_low, keep_high = position()
    loads = [
        pltpu.make_async_copy(source, target, in_sem.at[i])
        for i, (source, target) in enumerate((
            (along_hbm, along), (x0_hbm, x0), (x1_hbm, x1), (f11_hbm, f11), (lam_hbm, lam), (q_hbm, q)))
    ]
    node_loads = [
        [pltpu.make_async_copy(u_hbm.at[n, f], u.at[n, f], u_sem.at[n, f]) for n in range(3)] for f in range(4)
    ]
    for load in node_loads[0] + loads[:1] + node_loads[1] + loads[1:5] + node_loads[2] + node_loads[3] + loads[5:]:
        load.start()

    edge = 2 * PLANE
    middle = pl.ds(edge, OWN)
    odd = lax.axis_index("space") % 2
    sides = ((near_hbm, 1 - odd), (across_hbm, odd))
    stores = []

    def store(source, target, sem):
        copy = pltpu.make_async_copy(source, target, sem)
        copy.start()
        stores.append(copy)

    def field(f):
        nu = DIFFUSIVITY if f == 3 else VISCOSITY
        return nu, (2.0, -2.0, 1.0, 1.0)[f], f ^ 1

    def fine_plane(ref, f, p, low):
        return ref[f, pl.ds((p - low) * PLANE, PLANE)]

    def depth(ref, f, p, low, high):
        near = [fine_plane(ref, f, p + o, low) for o in (-1, 1) if low <= p + o < high]
        far = [fine_plane(ref, f, p + o, low) for o in (-2, 2) if low <= p + o < high]
        if not near:
            return -total(far)
        return 16.0 * total(near) - total(far) if far else 16.0 * total(near)

    def along_x(x):
        high, low = halves(x)
        return dot(high, along[...]) + dot(low, along[...])

    def combine(f):
        for load in node_loads[f]:
            load.wait()
        a_s[f] = (5.0 / 24.0) * u[0, f] + (1.0 / 3.0) * u[1, f] - (1.0 / 24.0) * u[2, f]

    def first_stage(f):
        nu, couple, partner = field(f)
        scale = nu * (SLAB_TIME / 12.0)
        row = along_x(a_s[f])
        for p in range(-2, FINE + 2):
            here = pl.ds((p + 2) * PLANE, PLANE)
            acc = depth(a_s, f, p, 0, FINE)
            if 0 <= p < FINE:
                own = pl.ds(p * PLANE, PLANE)
                centre = a_s[f, own]
                start = u[0, f, own]
                acc = acc + (across_y(centre) - 60.0 * centre) + row[p * PLANE:(p + 1) * PLANE]
                value = scale * acc + (couple * SLAB_TIME) * a_s[partner, own] + start
                if f == 3:
                    value = value + HALF_TIME * q[own]
                be[f, here] = 0.5 * value + ((-1.0 / 24.0) * start - (1.0 / 6.0) * u[1, f, own] + (5.0 / 24.0) * u[2, f, own])
            else:
                value = (scale * (keep_low if p < 0 else keep_high)) * acc
                be[f, here] = 0.5 * value
            fe[f, here] = value
        store(fe.at[f, middle], first_hbm.at[f], out_sem.at[f, 0])
        for i, (target, up) in enumerate(sides):
            rows = pl.ds(pl.multiple_of(up * (edge + OWN), edge), edge)
            store(fe.at[f, rows], target.at[f, pl.ds(0, edge)], out_sem.at[f, 1 + i])

    def second_stage(f):
        nu, couple, partner = field(f)
        scale = nu * (SLAB_TIME / 12.0)
        row = along_x(be[f])
        for p in range(-4, FINE + 4):
            here = pl.ds((p + 4) * PLANE, PLANE)
            acc = depth(be, f, p, -2, FINE + 2)
            mask = keep_low if p < 0 else keep_high
            if -2 <= p < FINE + 2:
                inner = pl.ds((p + 2) * PLANE, PLANE)
                centre = be[f, inner]
                first = fe[f, inner]
                acc = acc + (across_y(centre) - 60.0 * centre) + row[(p + 2) * PLANE:(p + 3) * PLANE]
                value = scale * acc + (couple * SLAB_TIME) * be[partner, inner] + first
                if 0 <= p < FINE:
                    own = pl.ds(p * PLANE, PLANE)
                    if f == 3:
                        value = value + HALF_TIME * q[own]
                    c = (1.0 / 6.0) * (value + u[0, f, own]) + (2.0 / 3.0) * first
                else:
                    value = mask * value
                    c = (1.0 / 6.0) * value + (2.0 / 3.0) * first
            else:
                value = (scale * mask) * acc
                c = (1.0 / 6.0) * value
            se[f, here] = value
            cs[f, here] = c
        store(se.at[f, pl.ds(2 * edge, OWN)], second_hbm.at[f], out_sem.at[f, 3])
        for i, (target, up) in enumerate(sides):
            rows = pl.ds(pl.multiple_of(up * (2 * edge + OWN), edge), 2 * edge)
            store(se.at[f, rows], target.at[f, pl.ds(edge, 2 * edge)], out_sem.at[f, 4 + i])

    def put(ref, f, k, value):
        for i in range(2):
            ref[f, i, pl.ds(k * PLANE, PLANE)] = value[:, i * 128:(i + 1) * 128]

    def every_other(ref, f, start, count):
        return jnp.concatenate([ref[f, i, pl.ds(start, count, stride=2), :] for i in range(2)], axis=1)

    def coarse_means(f):
        nu, couple, partner = field(f)
        scale = nu * (SLAB_TIME / 12.0)

        def pair_sum(ref, g, k):
            return fine_plane(ref, g, 2 * k, -4) + fine_plane(ref, g, 2 * k + 1, -4)

        for k in range(-3, COARSE + 3):
            value = None
            inside = -2 <= k < COARSE + 2
            if inside:
                mean = pair_sum(cs, f, k)
                put(pair_s, f, k + 2, mean)
                value = (-7.0 * scale) * mean + (couple * (SLAB_TIME * 0.5)) * pair_sum(cs, partner, k)
            for weight, planes in ((7.5, (2 * k - 1, 2 * k + 2)), (-0.5, (2 * k - 2, 2 * k + 3))):
                part = [fine_plane(cs, f, p, -4) for p in planes if -4 <= p < FINE + 4]
                if part:
                    part = (weight * scale) * total(part)
                    value = part if value is None else value + part
            if f == 3 and 0 <= k < COARSE:
                value = value + (0.5 * SLAB_TIME) * (q[pl.ds(2 * k * PLANE, PLANE)] + q[pl.ds((2 * k + 1) * PLANE, PLANE)])
            if k < 0:
                value = keep_low * value
            if k >= COARSE:
                value = keep_high * value
            if inside:
                last = 0.5 * pair_sum(se, f, k)
                value = value - last
                if 0 <= k < COARSE:
                    start = 0.5 * (u[0, f, pl.ds(2 * k * PLANE, PLANE)] + u[0, f, pl.ds((2 * k + 1) * PLANE, PLANE)])
                    value = value + start
                    last = last - mu * start
                    put(rows_s, f, 18 + k, start)
                put(rows_s, f, 12 + k, last)
            put(rows_s, f, k + 3, value)

    def across(f):
        nu, _, _ = field(f)
        scale = nu * (SLAB_TIME / 12.0)
        count = 22 * CY
        y = 0.5 * (every_other(rows_s, f, 0, count) + every_other(rows_s, f, 1, count))
        even = every_other(pair_s, f, 0, 8 * CY)
        odd = every_other(pair_s, f, 1, 8 * CY)
        mean = even + odd
        curved = []
        for k in range(8):
            rows = slice(k * CY, (k + 1) * CY)
            e, o = even[rows], odd[rows]
            near = rolled(o, 1, 0) + rolled(e, -1, 0)
            far = rolled(e, 1, 0) + rolled(o, -1, 0)
            value = (0.25 * scale) * (15.0 * near - far - 14.0 * mean[rows])
            if k < 2:
                value = keep_low * value
            if k >= 6:
                value = keep_high * value
            curved.append(value)
        y = jnp.concatenate([y[:CY], y[CY:9 * CY] + jnp.concatenate(curved, axis=0), y[9 * CY:]], axis=0)
        both = right(y, x0)
        bent = (0.25 * scale) * right(mean, x1)
        return jnp.concatenate([both[:CY], both[CY:9 * CY] + bent, both[9 * CY:]], axis=0)

    def to_y_modes(pair):
        both = jnp.concatenate([across(f) for f in pair], axis=1)
        half = PLANES * CY
        out = [left_stacked(f11[...], both[i * half:(i + 1) * half]) for i in range(2)]
        out = jnp.concatenate(out, axis=0)
        for i, f in enumerate(pair):
            lanes = slice(i * CX, (i + 1) * CX)
            w_s[f] = out[:18 * CY, lanes]
            y_s[f] = out[18 * CY:, lanes]

    def kept(value, p, count):
        if p < 0:
            return value * keep_low
        if p >= count:
            return value * keep_high
        return value

    def plane(ref, f, k, low, high):
        if low <= k < high:
            return ref[f, pl.ds((k - low) * CY, CY)]
        return None

    def node_plane(f, k):
        if -2 <= k < COARSE + 2:
            return w_s[f, pl.ds((12 + k) * CY, CY)]
        return None

    def coarse_slope(ref, f, k, low, high):
        nu, couple, partner = field(f)
        out = None
        for weight, offsets in ((16.0 / 48.0, (-1, 1)), (-1.0 / 48.0, (-2, 2))):
            part = [plane(ref, f, k + o, low, high) for o in offsets]
            part = [value for value in part if value is not None]
            if part:
                part = weight * total(part)
                out = part if out is None else out + part
        centre = plane(ref, f, k, low, high)
        if centre is None:
            return nu * out
        out = out + (lam[...] - 30.0 / 48.0) * centre
        return nu * out + couple * plane(ref, partner, k, low, high)

    def defect(f):
        for k in range(-2, COARSE + 2):
            value = coarse_slope(y_s, f, k, 0, COARSE)
            value = kept((mu * SLAB_TIME) * value, k, COARSE)
            rows = pl.ds((k + 3) * CY, CY)
            w_s[f, rows] = w_s[f, rows] - value

    def packet(f):
        for k in range(-SPILL, 16 - SPILL):
            rows = pl.ds((k + SPILL) * CY, CY)
            if k >= COARSE + SPILL:
                g_s[f, rows] = jnp.zeros((CY, CX), F32)
                continue
            value = kept(HALF_TIME * coarse_slope(w_s, f, k, -3, COARSE + 3), k, COARSE)
            for part in (plane(w_s, f, k, -3, COARSE + 3), node_plane(f, k)):
                if part is not None:
                    value = value + part
            g_s[f, rows] = value

    for pair in ((0, 1), (2, 3)):
        for f in pair:
            combine(f)
        if pair[0] == 0:
            loads[0].wait()
        else:
            loads[5].wait()
        for f in pair:
            first_stage(f)
        for f in pair:
            second_stage(f)
        for f in pair:
            coarse_means(f)
        if pair[0] == 0:
            for load in loads[1:5]:
                load.wait()
        to_y_modes(pair)
        for stage in (defect, packet):
            for f in pair:
                stage(f)

    def pack(p):
        values = []
        for half in range(2):
            for f in range(4):
                values.append(g_s[f, pl.ds(half * 8 * CY + p, 8, stride=CY), :])
        for t, value in enumerate(chunk_transpose(values)):
            send_s[t, p] = value

    step = BLOCKS // 4
    for i in range(4):
        for p in range(i * step, (i + 1) * step):
            pack(p)
        part = pl.ds(i * step, step)
        store(send_s.at[:, part], send_hbm.at[:, part], send_sem.at[i])
    for copy in stores:
        copy.wait()


def mode_kernel(g, xy, lam_z, lanes, zf, zb, out):
    index = lax.axis_index("tm") * BLOCKS + lax.axis_index("space")
    lam = lam_z[...] + xy[pl.ds(index, 1)]
    nu, other, couple, product = (lanes[pl.ds(i, 1)] for i in range(4))
    own = nu * lam
    partner = other * lam
    half_square = 0.5 * SLAB_TIME * SLAB_TIME
    diagonal = 1.0 + SLAB_TIME * own + half_square * (own * own + product)
    mixing = couple * (SLAB_TIME + half_square * (own + partner))
    lane = lax.broadcasted_iota(jnp.int32, (CZ, 128), 1)
    even = (lane & CHUNK) == 0
    left_half = lane < 64

    state = None
    states = [jnp.zeros((CZ, 128), F32)]
    for s in range(SLABS):
        both = left(zf, g[pl.ds(s * BLOCKS * 8, BLOCKS * 8)])
        source = both[:CZ] + rolled(both[CZ:], 64, 1)
        if state is None:
            state = source
        else:
            swapped = jnp.where(even, rolled(state, -CHUNK, 1), rolled(state, CHUNK, 1))
            state = diagonal * state + mixing * swapped + source
        state = jnp.where(left_half, state, 0.0)
        states.append(state)
    for s in range(SLABS):
        packed = states[s] + rolled(states[s + 1], 64, 1)
        out[pl.ds(s * CZ, CZ)] = left(zb, packed)


def paired(x, axis):
    index = lax.broadcasted_iota(jnp.int32, x.shape, axis)
    return x + jnp.where((index & 1) == 0, rolled(x, -1, axis), rolled(x, 1, axis))


def block_mean(x, weight):
    return paired(paired(weight * x, 0), 1)


def middle_kernel(first_hbm, near_hbm, across_hbm, most_hbm, rest_hbm, u_hbm, first_out, second_out,
                  first, spill, second, u, out, in_sem, out_sem):
    mu, _, _ = position()
    odd = lax.axis_index("space") % 2
    part = pl.ds(0, 2 * PLANE)
    loads = []
    for f in range(4):
        source = most_hbm.at[f] if f < SENT_FIRST else rest_hbm.at[f - SENT_FIRST]
        moves = ((first_hbm.at[f], first.at[f]), (near_hbm.at[f, part], spill.at[0, f]), (across_hbm.at[f, part], spill.at[1, f]),
                 (source, second.at[f]), (u_hbm.at[0, f], u.at[f]))
        for i, (source, target) in enumerate(moves):
            load = pltpu.make_async_copy(source, target, in_sem.at[f, i])
            load.start()
            loads.append(load)
    stores = []
    for f in range(4):
        for load in loads[5 * f:5 * f + 5]:
            load.wait()
        for k in range(COARSE):
            pair = [pl.ds((2 * k + i) * PLANE, PLANE) for i in range(2)]
            seconds = [second[f, rows] for rows in pair]
            mean = block_mean(seconds[0] + seconds[1], 0.125)
            start = block_mean(u[f, pair[0]] + u[f, pair[1]], 0.125 * mu)
            middle = 0.5 * (mean + start)
            for i, rows in enumerate(pair):
                p = 2 * k + i
                value = first[f, rows] - middle
                if p < 2:
                    value = value + spill[1 - odd, f, pl.ds(p * PLANE, PLANE)]
                if p >= FINE - 2:
                    value = value + spill[odd, f, pl.ds((p - FINE + 2) * PLANE, PLANE)]
                out[0, f, rows] = value
                out[1, f, rows] = seconds[i] - mean
        for n, target in enumerate((first_out, second_out)):
            store = pltpu.make_async_copy(out.at[n, f], target.at[f], out_sem.at[n, f])
            store.start()
            stores.append(store)
    for store in stores:
        store.wait()


def doubled(x):
    return jnp.concatenate([x[(p // 2) * PLANE:(p // 2 + 1) * PLANE] for p in range(FINE)], axis=0)


def nodes_kernel(modes, first_hbm, second_hbm, most_hbm, rest_hbm, yb_hbm, xb_hbm, u_hbm, out, h_s, first, second, before, yb, xb, p_s, out_s, in_sem, sem):
    mu, _, _ = position()
    leading = lax.axis_index("tm") == 0
    tables = [pltpu.make_async_copy(yb_hbm, yb, in_sem.at[0, 3]), pltpu.make_async_copy(xb_hbm, xb, in_sem.at[1, 3])]
    for load in tables:
        load.start()
    for f in range(4):
        for i, (source, target) in enumerate(((first_hbm, first), (second_hbm, second))):
            pltpu.make_async_copy(source.at[f], target.at[f], in_sem.at[f, i]).start()

        @pl.when(leading)
        def _():
            pltpu.make_async_copy(u_hbm.at[0, f], before.at[f], in_sem.at[f, 2]).start()

        @pl.when(jnp.logical_not(leading))
        def _():
            source = most_hbm.at[f] if f < SENT_FIRST else rest_hbm.at[f - SENT_FIRST]
            pltpu.make_async_copy(source, before.at[f], in_sem.at[f, 2]).start()

    for r in range(8):
        values = [modes[pl.ds(t * 64 + r * 8, 8)] for t in range(SLABS)]
        for g, value in enumerate(chunk_transpose(values)):
            h_s[g, pl.ds(r * 8, 8)] = value
    for load in tables:
        load.wait()
    for g in range(8):
        p_s[g] = right(left(yb, h_s[g]), xb)
    stores = []
    for f in range(4):
        start = p_s[f]
        end = p_s[4 + f]
        for i, (source, target) in enumerate(((first_hbm, first), (second_hbm, second), (second_hbm, before))):
            pltpu.make_async_copy(source.at[f], target.at[f], in_sem.at[f, i]).wait()
        for k in range(COARSE):
            pair = [pl.ds((2 * k + i) * PLANE, PLANE) for i in range(2)]
            value = [before[f, rows] for rows in pair]
            shift = start[k * PLANE:(k + 1) * PLANE] - block_mean(value[0] + value[1], 0.125 * mu)
            for i, rows in enumerate(pair):
                out_s[0, f, rows] = value[i] + shift
        out_s[1, f] = first[f] + doubled(0.5 * (start + end))
        out_s[2, f] = second[f] + doubled(end)
        for n in range(3):
            store = pltpu.make_async_copy(out_s.at[n, f], out.at[n, f], sem.at[n, f])
            store.start()
            stores.append(store)
    for store in stores:
        store.wait()


VM = pl.BlockSpec(memory_space=pltpu.VMEM)
ANY = pl.BlockSpec(memory_space=pl.ANY)


GRANT = 60
SENT_FIRST = 3
MODE_COST = 20
MIDDLE_COST = 3


def params(mib):
    return pltpu.CompilerParams(vmem_limit_bytes=mib << 20)


def cost(microseconds):
    return pl.CostEstimate(flops=int(microseconds * 1e9), bytes_accessed=0, transcendentals=0)


def shape(*sizes):
    return jax.ShapeDtypeStruct(sizes, F32)


def scratch(*sizes):
    return pltpu.VMEM(sizes, F32)


def like(constant):
    return pltpu.VMEM(constant.shape, constant.dtype)


def per_device(fine_nodes, heating):
    u = fine_nodes.reshape(3, 4, OWN, NX)
    heat = heating.reshape(OWN, NX)
    field = (4, OWN, NX)
    spill = (4, 6 * PLANE, NX)
    near = (4, 2 * PLANE, NX)
    tables = (ALONG, F11, X0, X1, LAM_XY)
    dma = pltpu.SemaphoreType.DMA

    with jax.named_scope("fine"):
        first_c, second_c, to_near, to_across, packet = pl.pallas_call(
            fine_kernel,
            out_shape=[shape(*field), shape(*field), shape(*spill), shape(*spill),
                       shape(SLABS, BLOCKS, 8, 128)],
            in_specs=[ANY] * (2 + len(tables)),
            out_specs=[ANY] * 5,
            scratch_shapes=[scratch(3, 4, OWN, NX), scratch(OWN, NX)] + [like(table) for table in tables] + [
                scratch(*field),
                scratch(4, 12 * PLANE, NX),
                scratch(4, 12 * PLANE, NX),
                scratch(4, 16 * PLANE, NX),
                scratch(4, 16 * PLANE, NX),
                scratch(4, 2, 22 * PLANE, 128),
                scratch(4, 2, 8 * PLANE, 128),
                scratch(4, 4 * CY, CX),
                scratch(4, 18 * CY, CX),
                scratch(4, 16 * CY, CX),
                scratch(SLABS, BLOCKS, 8, 128),
                dma((6,)), dma((3, 4)), dma((4, 6)), dma((4,)),
            ],
            compiler_params=params(GRANT),
        )(u, heat, *tables)

    with jax.named_scope("to_modes"):
        modes = lax.all_to_all(packet.reshape(SLABS * BLOCKS, 8, 128), AXES, 0, 0, tiled=True)

    with jax.named_scope("spill"):
        chip = [(i, i ^ 1) for i in range(BLOCKS)]
        chips = [(i, i + 1) for i in range(1, BLOCKS - 1, 2)]
        from_near = lax.ppermute(to_near, "space", chip)
        from_across = lax.ppermute(to_across, "space", chips + [(j, i) for i, j in chips])

    with jax.named_scope("end"):
        odd = lax.axis_index("space") % 2 == 1
        far = slice(2 * PLANE, 6 * PLANE)

        def ended(fields):
            near, across = from_near[fields, far], from_across[fields, far]
            return second_c[fields] + jnp.concatenate([jnp.where(odd, near, across), jnp.where(odd, across, near)], axis=1)

        most = ended(slice(0, SENT_FIRST))
        rest = ended(slice(SENT_FIRST, 4))

    with jax.named_scope("pass"):
        later = [(i, i + 1) for i in range(SLABS - 1)]
        most_before = lax.ppermute(most, "tm", later)

    with jax.named_scope("modes"):
        constants = (MODE_XY, LAM_Z_COLUMN, LANES, ZF, ZB)
        solved = pl.pallas_call(
            mode_kernel,
            out_shape=shape(SLABS * CZ, 128),
            in_specs=[VM] * 6,
            out_specs=VM,
            cost_estimate=cost(MODE_COST),
            compiler_params=params(16),
        )(modes.reshape(SLABS * BLOCKS * 8, 128), *constants)

    with jax.named_scope("pass_rest"):
        rest_sent, _ = lax.optimization_barrier((rest, solved))
        rest_before = lax.ppermute(rest_sent, "tm", later)

    with jax.named_scope("middle"):
        first, second = pl.pallas_call(
            middle_kernel,
            out_shape=[shape(*field)] * 2,
            in_specs=[ANY] * 6,
            out_specs=[ANY] * 2,
            scratch_shapes=[scratch(*field), scratch(2, *near), scratch(*field), scratch(*field), scratch(2, *field),
                            dma((4, 5)), dma((2, 4))],
            cost_estimate=cost(MIDDLE_COST),
            compiler_params=params(GRANT),
        )(first_c, from_near, from_across, most, rest, u)

    with jax.named_scope("from_modes"):
        solved = solved.reshape(SLABS * BLOCKS, COARSE, 128)
        back = lax.all_to_all(solved, AXES, 0, 0, tiled=True).reshape(SLABS * CZ, 128)

    with jax.named_scope("nodes"):
        out = pl.pallas_call(
            nodes_kernel,
            out_shape=shape(3, *field),
            in_specs=[VM] + [ANY] * 7,
            out_specs=ANY,
            scratch_shapes=[scratch(8, 64, 128)] + [scratch(*field)] * 3 + [like(YB), like(XB), scratch(8, OWN // 2, NX), scratch(3, *field), dma((4, 4)), dma((3, 4))],
            cost_estimate=cost(5),
            compiler_params=params(GRANT),
        )(back, first, second, most_before, rest_before, YB, XB, u)
    return out.reshape(1, 3, 4, FINE, NY, NX)


def solution(mesh):
    in_specs = (P("tm", None, None, "space", None, None), P("space", None, None))
    out_specs = P("tm", None, None, "space", None, None)
    return jax.shard_map(
        per_device, mesh=mesh, in_specs=in_specs, out_specs=out_specs, check_vma=False
    )
```

```python
import numpy as np
import jax
import jax.numpy as jnp
from jax import lax
from jax.experimental import pallas as pl
from jax.experimental.pallas import tpu as pltpu
from jax.sharding import PartitionSpec as P

VISCOSITY = 0.4
DIFFUSIVITY = 0.3
SLAB_TIME = 0.25
HALF_TIME = 0.125

SLABS = 8
BLOCKS = 16
NZ, NY, NX = 128, 32, 256
CZ, CY, CX = NZ // 2, NY // 2, NX // 2
FINE = NZ // BLOCKS
COARSE = CZ // BLOCKS
CHUNK = CX // SLABS
SPILL = 5
AXES = ("tm", "space")
F32 = jnp.float32
BF16 = jnp.bfloat16


def real_basis(count):
    j = np.arange(count)
    rows, values = [], []
    for k in range(count):
        theta = 2.0 * np.pi * k / count
        if k == 0:
            row = np.ones(count)
        elif 2 * k == count:
            row = np.cos(np.pi * j)
        elif 2 * k < count:
            row = np.cos(theta * j) * np.sqrt(2.0)
        else:
            row = np.sin(theta * j) * np.sqrt(2.0)
        rows.append(row / np.sqrt(count))
        values.append((32.0 * np.cos(theta) - 2.0 * np.cos(2.0 * theta) - 30.0) / 48.0)
    return np.array(rows), np.array(values)


def pairs(count):
    return np.repeat(np.eye(count), 2, axis=0)


def circulant(count):
    eye = np.eye(count)
    return (
        16.0 * (np.roll(eye, 1, 0) + np.roll(eye, -1, 0))
        - (np.roll(eye, 2, 0) + np.roll(eye, -2, 0))
        - 30.0 * eye
    )


def split(matrix):
    matrix = np.asarray(matrix, np.float32)
    high = matrix.astype(jnp.bfloat16)
    low = (matrix - high.astype(np.float32)).astype(jnp.bfloat16)
    return np.stack([high, low])


FY, LAM_Y = real_basis(CY)
FX, LAM_X = real_basis(CX)


def depth_basis():
    eye = np.eye(CZ)
    band = -30.0 * eye
    for offset, weight in ((1, 16.0), (2, -1.0)):
        band += weight * (np.eye(CZ, k=offset) + np.eye(CZ, k=-offset))
    values, vectors = np.linalg.eigh(band / 48.0)
    return values, vectors


LAM_Z, QZ = depth_basis()

DOWN_X = (FX @ pairs(CX).T * 0.5).T
DOWN_XL = circulant(NX) @ DOWN_X
UP_Y = pairs(CY) @ FY.T
UP_X = FX @ pairs(CX).T


def exact(matrix):
    high = np.asarray(matrix, np.float32).astype(jnp.bfloat16)
    assert np.array_equal(high.astype(np.float64), matrix)
    return high


def stacked(matrix):
    return split(matrix).reshape(-1, matrix.shape[1])


ALONG = exact(circulant(NX))
PLANES = 11
F11 = stacked(np.kron(np.eye(PLANES), FY))
X0 = split(DOWN_X)
X1 = split(DOWN_XL)
LAM_XY = (LAM_Y[:, None] + LAM_X[None, :]).astype(np.float32)


def depth_forward():
    table = np.zeros((2, CZ, BLOCKS, 8))
    for half in range(2):
        for block in range(BLOCKS):
            for slot in range(8):
                z = block * COARSE + half * 8 + slot - SPILL
                if 0 <= z < CZ:
                    table[half, :, block, slot] = QZ[z]
    return table.reshape(2 * CZ, BLOCKS * 8)


ZF = split(depth_forward())
ZB = split(QZ)


def up_y_table():
    table = np.zeros((COARSE, NY, CY, COARSE))
    for z in range(COARSE):
        table[z, :, :, z] = UP_Y
    return table.reshape(COARSE * NY, CY * COARSE)


YB = split(up_y_table())
XB = split(UP_X)


def mode_values():
    table = np.zeros((SLABS, BLOCKS, 2, 4, CHUNK))
    for t in range(SLABS):
        for p in range(BLOCKS):
            table[t, p] = LAM_Y[p] + LAM_X[t * CHUNK:(t + 1) * CHUNK]
    return table.reshape(SLABS * BLOCKS, 128).astype(np.float32)


def lane_constants():
    own = np.array([VISCOSITY, VISCOSITY, VISCOSITY, DIFFUSIVITY])
    partner = np.array([VISCOSITY, VISCOSITY, DIFFUSIVITY, VISCOSITY])
    couple = np.array([2.0, -2.0, 1.0, 1.0])
    product = np.array([-4.0, -4.0, 1.0, 1.0])
    table = np.zeros((8, 2, 4, CHUNK))
    for row, values in enumerate((own, partner, couple, product)):
        table[row] = values[None, :, None]
    return table.reshape(8, 128).astype(np.float32)


MODE_XY = mode_values()
LANES = lane_constants()
LAM_Z_COLUMN = np.repeat(LAM_Z[:, None], 128, axis=1).astype(np.float32)


def halves(x):
    high = x.astype(BF16)
    return high, (x - high.astype(F32)).astype(BF16)


def dot(a, b):
    return jnp.dot(a, b, preferred_element_type=F32)


def left(table, x):
    high, low = halves(x)
    return dot(table[0], high) + (dot(table[0], low) + dot(table[1], high))


def right(x, table):
    high, low = halves(x)
    return dot(high, table[0]) + (dot(low, table[0]) + dot(high, table[1]))


def rolled(x, by, axis):
    return pltpu.roll(x, by % x.shape[axis], axis)


def across_y(x):
    near = rolled(x, 1, 0) + rolled(x, -1, 0)
    far = rolled(x, 2, 0) + rolled(x, -2, 0)
    return 16.0 * near - far


def total(terms):
    out = terms[0]
    for term in terms[1:]:
        out = out + term
    return out


def chunk_transpose(values):
    values = list(values)
    lane = lax.broadcasted_iota(jnp.int32, values[0].shape, 1)
    for bit in (1, 2, 4):
        shift = CHUNK * bit
        low = (lane & shift) == 0
        for i in range(8):
            if i & bit:
                continue
            j = i | bit
            first, second = values[i], values[j]
            values[i] = jnp.where(low, first, rolled(second, shift, 1))
            values[j] = jnp.where(low, rolled(first, -shift, 1), second)
    return values


def left_stacked(table, x):
    high, low = halves(x)
    rows = table.shape[0] // 2
    both = dot(table, high)
    return both[:rows] + (both[rows:] + dot(table[:rows], low))


PLANE = NY
OWN = FINE * PLANE


def position():
    tm, space = lax.axis_index("tm"), lax.axis_index("space")
    one = jnp.float32(1.0)
    zero = jnp.float32(0.0)
    return jnp.where(tm > 0, one, zero), jnp.where(space > 0, one, zero), jnp.where(space < BLOCKS - 1, one, zero)


def fine_kernel(u_hbm, q_hbm, along_hbm, f11_hbm, x0_hbm, x1_hbm, lam_hbm,
                first_hbm, second_hbm, near_hbm, across_hbm, send_hbm,
                u, q, along, f11, x0, x1, lam,
                a_s, fe, be, se, cs, rows_s, pair_s, y_s, w_s, g_s, send_s, in_sem, u_sem, out_sem, send_sem):
    mu, keep_low, keep_high = position()
    loads = [
        pltpu.make_async_copy(source, target, in_sem.at[i])
        for i, (source, target) in enumerate((
            (along_hbm, along), (x0_hbm, x0), (x1_hbm, x1), (f11_hbm, f11), (lam_hbm, lam), (q_hbm, q)))
    ]
    node_loads = [
        [pltpu.make_async_copy(u_hbm.at[n, f], u.at[n, f], u_sem.at[n, f]) for n in range(3)] for f in range(4)
    ]
    for load in node_loads[0] + loads[:1] + node_loads[1] + loads[1:5] + node_loads[2] + node_loads[3] + loads[5:]:
        load.start()

    edge = 2 * PLANE
    middle = pl.ds(edge, OWN)
    odd = lax.axis_index("space") % 2
    sides = ((near_hbm, 1 - odd), (across_hbm, odd))
    stores = []

    def store(source, target, sem):
        copy = pltpu.make_async_copy(source, target, sem)
        copy.start()
        stores.append(copy)

    def field(f):
        nu = DIFFUSIVITY if f == 3 else VISCOSITY
        return nu, (2.0, -2.0, 1.0, 1.0)[f], f ^ 1

    def fine_plane(ref, f, p, low):
        return ref[f, pl.ds((p - low) * PLANE, PLANE)]

    def depth(ref, f, p, low, high):
        near = [fine_plane(ref, f, p + o, low) for o in (-1, 1) if low <= p + o < high]
        far = [fine_plane(ref, f, p + o, low) for o in (-2, 2) if low <= p + o < high]
        if not near:
            return -total(far)
        return 16.0 * total(near) - total(far) if far else 16.0 * total(near)

    def along_x(x):
        high, low = halves(x)
        return dot(high, along[...]) + dot(low, along[...])

    def combine(f):
        for load in node_loads[f]:
            load.wait()
        a_s[f] = (5.0 / 24.0) * u[0, f] + (1.0 / 3.0) * u[1, f] - (1.0 / 24.0) * u[2, f]

    def first_stage(f):
        nu, couple, partner = field(f)
        scale = nu * (SLAB_TIME / 12.0)
        row = along_x(a_s[f])
        for p in range(-2, FINE + 2):
            here = pl.ds((p + 2) * PLANE, PLANE)
            acc = depth(a_s, f, p, 0, FINE)
            if 0 <= p < FINE:
                own = pl.ds(p * PLANE, PLANE)
                centre = a_s[f, own]
                start = u[0, f, own]
                acc = acc + (across_y(centre) - 60.0 * centre) + row[p * PLANE:(p + 1) * PLANE]
                value = scale * acc + (couple * SLAB_TIME) * a_s[partner, own] + start
                if f == 3:
                    value = value + HALF_TIME * q[own]
                be[f, here] = 0.5 * value + ((-1.0 / 24.0) * start - (1.0 / 6.0) * u[1, f, own] + (5.0 / 24.0) * u[2, f, own])
            else:
                value = (scale * (keep_low if p < 0 else keep_high)) * acc
                be[f, here] = 0.5 * value
            fe[f, here] = value
        store(fe.at[f, middle], first_hbm.at[f], out_sem.at[f, 0])
        for i, (target, up) in enumerate(sides):
            rows = pl.ds(pl.multiple_of(up * (edge + OWN), edge), edge)
            store(fe.at[f, rows], target.at[f, pl.ds(0, edge)], out_sem.at[f, 1 + i])

    def second_stage(f):
        nu, couple, partner = field(f)
        scale = nu * (SLAB_TIME / 12.0)
        row = along_x(be[f])
        for p in range(-4, FINE + 4):
            here = pl.ds((p + 4) * PLANE, PLANE)
            acc = depth(be, f, p, -2, FINE + 2)
            mask = keep_low if p < 0 else keep_high
            if -2 <= p < FINE + 2:
                inner = pl.ds((p + 2) * PLANE, PLANE)
                centre = be[f, inner]
                first = fe[f, inner]
                acc = acc + (across_y(centre) - 60.0 * centre) + row[(p + 2) * PLANE:(p + 3) * PLANE]
                value = scale * acc + (couple * SLAB_TIME) * be[partner, inner] + first
                if 0 <= p < FINE:
                    own = pl.ds(p * PLANE, PLANE)
                    if f == 3:
                        value = value + HALF_TIME * q[own]
                    c = (1.0 / 6.0) * (value + u[0, f, own]) + (2.0 / 3.0) * first
                else:
                    value = mask * value
                    c = (1.0 / 6.0) * value + (2.0 / 3.0) * first
            else:
                value = (scale * mask) * acc
                c = (1.0 / 6.0) * value
            se[f, here] = value
            cs[f, here] = c
        store(se.at[f, pl.ds(2 * edge, OWN)], second_hbm.at[f], out_sem.at[f, 3])
        for i, (target, up) in enumerate(sides):
            rows = pl.ds(pl.multiple_of(up * (2 * edge + OWN), edge), 2 * edge)
            store(se.at[f, rows], target.at[f, pl.ds(edge, 2 * edge)], out_sem.at[f, 4 + i])

    def put(ref, f, k, value):
        for i in range(2):
            ref[f, i, pl.ds(k * PLANE, PLANE)] = value[:, i * 128:(i + 1) * 128]

    def every_other(ref, f, start, count):
        return jnp.concatenate([ref[f, i, pl.ds(start, count, stride=2), :] for i in range(2)], axis=1)

    def coarse_means(f):
        nu, couple, partner = field(f)
        scale = nu * (SLAB_TIME / 12.0)

        def pair_sum(ref, g, k):
            return fine_plane(ref, g, 2 * k, -4) + fine_plane(ref, g, 2 * k + 1, -4)

        for k in range(-3, COARSE + 3):
            value = None
            inside = -2 <= k < COARSE + 2
            if inside:
                mean = pair_sum(cs, f, k)
                put(pair_s, f, k + 2, mean)
                value = (-7.0 * scale) * mean + (couple * (SLAB_TIME * 0.5)) * pair_sum(cs, partner, k)
            for weight, planes in ((7.5, (2 * k - 1, 2 * k + 2)), (-0.5, (2 * k - 2, 2 * k + 3))):
                part = [fine_plane(cs, f, p, -4) for p in planes if -4 <= p < FINE + 4]
                if part:
                    part = (weight * scale) * total(part)
                    value = part if value is None else value + part
            if f == 3 and 0 <= k < COARSE:
                value = value + (0.5 * SLAB_TIME) * (q[pl.ds(2 * k * PLANE, PLANE)] + q[pl.ds((2 * k + 1) * PLANE, PLANE)])
            if k < 0:
                value = keep_low * value
            if k >= COARSE:
                value = keep_high * value
            if inside:
                last = 0.5 * pair_sum(se, f, k)
                value = value - last
                if 0 <= k < COARSE:
                    start = 0.5 * (u[0, f, pl.ds(2 * k * PLANE, PLANE)] + u[0, f, pl.ds((2 * k + 1) * PLANE, PLANE)])
                    value = value + start
                    last = last - mu * start
                    put(rows_s, f, 18 + k, start)
                put(rows_s, f, 12 + k, last)
            put(rows_s, f, k + 3, value)

    def across(f):
        nu, _, _ = field(f)
        scale = nu * (SLAB_TIME / 12.0)
        count = 22 * CY
        y = 0.5 * (every_other(rows_s, f, 0, count) + every_other(rows_s, f, 1, count))
        even = every_other(pair_s, f, 0, 8 * CY)
        odd = every_other(pair_s, f, 1, 8 * CY)
        mean = even + odd
        curved = []
        for k in range(8):
            rows = slice(k * CY, (k + 1) * CY)
            e, o = even[rows], odd[rows]
            near = rolled(o, 1, 0) + rolled(e, -1, 0)
            far = rolled(e, 1, 0) + rolled(o, -1, 0)
            value = (0.25 * scale) * (15.0 * near - far - 14.0 * mean[rows])
            if k < 2:
                value = keep_low * value
            if k >= 6:
                value = keep_high * value
            curved.append(value)
        y = jnp.concatenate([y[:CY], y[CY:9 * CY] + jnp.concatenate(curved, axis=0), y[9 * CY:]], axis=0)
        both = right(y, x0)
        bent = (0.25 * scale) * right(mean, x1)
        return jnp.concatenate([both[:CY], both[CY:9 * CY] + bent, both[9 * CY:]], axis=0)

    def to_y_modes(pair):
        both = jnp.concatenate([across(f) for f in pair], axis=1)
        half = PLANES * CY
        out = [left_stacked(f11[...], both[i * half:(i + 1) * half]) for i in range(2)]
        out = jnp.concatenate(out, axis=0)
        for i, f in enumerate(pair):
            lanes = slice(i * CX, (i + 1) * CX)
            w_s[f] = out[:18 * CY, lanes]
            y_s[f] = out[18 * CY:, lanes]

    def kept(value, p, count):
        if p < 0:
            return value * keep_low
        if p >= count:
            return value * keep_high
        return value

    def plane(ref, f, k, low, high):
        if low <= k < high:
            return ref[f, pl.ds((k - low) * CY, CY)]
        return None

    def node_plane(f, k):
        if -2 <= k < COARSE + 2:
            return w_s[f, pl.ds((12 + k) * CY, CY)]
        return None

    def coarse_slope(ref, f, k, low, high):
        nu, couple, partner = field(f)
        out = None
        for weight, offsets in ((16.0 / 48.0, (-1, 1)), (-1.0 / 48.0, (-2, 2))):
            part = [plane(ref, f, k + o, low, high) for o in offsets]
            part = [value for value in part if value is not None]
            if part:
                part = weight * total(part)
                out = part if out is None else out + part
        centre = plane(ref, f, k, low, high)
        if centre is None:
            return nu * out
        out = out + (lam[...] - 30.0 / 48.0) * centre
        return nu * out + couple * plane(ref, partner, k, low, high)

    def defect(f):
        for k in range(-2, COARSE + 2):
            value = coarse_slope(y_s, f, k, 0, COARSE)
            value = kept((mu * SLAB_TIME) * value, k, COARSE)
            rows = pl.ds((k + 3) * CY, CY)
            w_s[f, rows] = w_s[f, rows] - value

    def packet(f):
        for k in range(-SPILL, 16 - SPILL):
            rows = pl.ds((k + SPILL) * CY, CY)
            if k >= COARSE + SPILL:
                g_s[f, rows] = jnp.zeros((CY, CX), F32)
                continue
            value = kept(HALF_TIME * coarse_slope(w_s, f, k, -3, COARSE + 3), k, COARSE)
            for part in (plane(w_s, f, k, -3, COARSE + 3), node_plane(f, k)):
                if part is not None:
                    value = value + part
            g_s[f, rows] = value

    for pair in ((0, 1), (2, 3)):
        for f in pair:
            combine(f)
        if pair[0] == 0:
            loads[0].wait()
        else:
            loads[5].wait()
        for f in pair:
            first_stage(f)
        for f in pair:
            second_stage(f)
        for f in pair:
            coarse_means(f)
        if pair[0] == 0:
            for load in loads[1:5]:
                load.wait()
        to_y_modes(pair)
        for stage in (defect, packet):
            for f in pair:
                stage(f)

    def pack(p):
        values = []
        for half in range(2):
            for f in range(4):
                values.append(g_s[f, pl.ds(half * 8 * CY + p, 8, stride=CY), :])
        for t, value in enumerate(chunk_transpose(values)):
            send_s[t, p] = value

    step = BLOCKS // 4
    for i in range(4):
        for p in range(i * step, (i + 1) * step):
            pack(p)
        part = pl.ds(i * step, step)
        store(send_s.at[:, part], send_hbm.at[:, part], send_sem.at[i])
    for copy in stores:
        copy.wait()


def mode_kernel(g, xy, lam_z, lanes, zf, zb, out):
    index = lax.axis_index("tm") * BLOCKS + lax.axis_index("space")
    lam = lam_z[...] + xy[pl.ds(index, 1)]
    nu, other, couple, product = (lanes[pl.ds(i, 1)] for i in range(4))
    own = nu * lam
    partner = other * lam
    half_square = 0.5 * SLAB_TIME * SLAB_TIME
    diagonal = 1.0 + SLAB_TIME * own + half_square * (own * own + product)
    mixing = couple * (SLAB_TIME + half_square * (own + partner))
    lane = lax.broadcasted_iota(jnp.int32, (CZ, 128), 1)
    even = (lane & CHUNK) == 0
    left_half = lane < 64

    state = None
    states = [jnp.zeros((CZ, 128), F32)]
    for s in range(SLABS):
        both = left(zf, g[pl.ds(s * BLOCKS * 8, BLOCKS * 8)])
        source = both[:CZ] + rolled(both[CZ:], 64, 1)
        if state is None:
            state = source
        else:
            swapped = jnp.where(even, rolled(state, -CHUNK, 1), rolled(state, CHUNK, 1))
            state = diagonal * state + mixing * swapped + source
        state = jnp.where(left_half, state, 0.0)
        states.append(state)
    for s in range(SLABS):
        packed = states[s] + rolled(states[s + 1], 64, 1)
        out[pl.ds(s * CZ, CZ)] = left(zb, packed)


def paired(x, axis):
    index = lax.broadcasted_iota(jnp.int32, x.shape, axis)
    return x + jnp.where((index & 1) == 0, rolled(x, -1, axis), rolled(x, 1, axis))


def block_mean(x, weight):
    return paired(paired(weight * x, 0), 1)


def middle_kernel(first_hbm, near_hbm, across_hbm, most_hbm, rest_hbm, u_hbm, first_out, second_out,
                  first, spill, second, u, out, in_sem, out_sem):
    mu, _, _ = position()
    odd = lax.axis_index("space") % 2
    part = pl.ds(0, 2 * PLANE)
    loads = []
    for f in range(4):
        source = most_hbm.at[f] if f < SENT_FIRST else rest_hbm.at[f - SENT_FIRST]
        moves = ((first_hbm.at[f], first.at[f]), (near_hbm.at[f, part], spill.at[0, f]), (across_hbm.at[f, part], spill.at[1, f]),
                 (source, second.at[f]), (u_hbm.at[0, f], u.at[f]))
        for i, (source, target) in enumerate(moves):
            load = pltpu.make_async_copy(source, target, in_sem.at[f, i])
            load.start()
            loads.append(load)
    stores = []
    for f in range(4):
        for load in loads[5 * f:5 * f + 5]:
            load.wait()
        for k in range(COARSE):
            pair = [pl.ds((2 * k + i) * PLANE, PLANE) for i in range(2)]
            seconds = [second[f, rows] for rows in pair]
            mean = block_mean(seconds[0] + seconds[1], 0.125)
            start = block_mean(u[f, pair[0]] + u[f, pair[1]], 0.125 * mu)
            middle = 0.5 * (mean + start)
            for i, rows in enumerate(pair):
                p = 2 * k + i
                value = first[f, rows] - middle
                if p < 2:
                    value = value + spill[1 - odd, f, pl.ds(p * PLANE, PLANE)]
                if p >= FINE - 2:
                    value = value + spill[odd, f, pl.ds((p - FINE + 2) * PLANE, PLANE)]
                out[0, f, rows] = value
                out[1, f, rows] = seconds[i] - mean
        for n, target in enumerate((first_out, second_out)):
            store = pltpu.make_async_copy(out.at[n, f], target.at[f], out_sem.at[n, f])
            store.start()
            stores.append(store)
    for store in stores:
        store.wait()


def doubled(x):
    return jnp.concatenate([x[(p // 2) * PLANE:(p // 2 + 1) * PLANE] for p in range(FINE)], axis=0)


def nodes_kernel(modes_hbm, first_hbm, second_hbm, most_hbm, rest_hbm, yb_hbm, xb_hbm, u_hbm, out, modes, h_s, first, second, before, yb, xb, p_s, out_s, in_sem, sem):
    mu, _, _ = position()
    leading = lax.axis_index("tm") == 0
    arrived = pltpu.make_async_copy(modes_hbm, modes, in_sem.at[2, 3])
    tables = [pltpu.make_async_copy(yb_hbm, yb, in_sem.at[0, 3]), pltpu.make_async_copy(xb_hbm, xb, in_sem.at[1, 3])]
    for load in [arrived] + tables:
        load.start()
    for f in range(4):
        for i, (source, target) in enumerate(((first_hbm, first), (second_hbm, second))):
            pltpu.make_async_copy(source.at[f], target.at[f], in_sem.at[f, i]).start()

        @pl.when(leading)
        def _():
            pltpu.make_async_copy(u_hbm.at[0, f], before.at[f], in_sem.at[f, 2]).start()

        @pl.when(jnp.logical_not(leading))
        def _():
            source = most_hbm.at[f] if f < SENT_FIRST else rest_hbm.at[f - SENT_FIRST]
            pltpu.make_async_copy(source, before.at[f], in_sem.at[f, 2]).start()

    arrived.wait()
    for r in range(8):
        values = [modes[pl.ds(t * 64 + r * 8, 8)] for t in range(SLABS)]
        for g, value in enumerate(chunk_transpose(values)):
            h_s[g, pl.ds(r * 8, 8)] = value
    for load in tables:
        load.wait()
    for g in range(8):
        p_s[g] = right(left(yb, h_s[g]), xb)
    stores = []
    for f in range(4):
        start = p_s[f]
        end = p_s[4 + f]
        for i, (source, target) in enumerate(((first_hbm, first), (second_hbm, second), (second_hbm, before))):
            pltpu.make_async_copy(source.at[f], target.at[f], in_sem.at[f, i]).wait()
        for k in range(COARSE):
            pair = [pl.ds((2 * k + i) * PLANE, PLANE) for i in range(2)]
            value = [before[f, rows] for rows in pair]
            shift = start[k * PLANE:(k + 1) * PLANE] - block_mean(value[0] + value[1], 0.125 * mu)
            for i, rows in enumerate(pair):
                out_s[0, f, rows] = value[i] + shift
        out_s[1, f] = first[f] + doubled(0.5 * (start + end))
        out_s[2, f] = second[f] + doubled(end)
        for n in range(3):
            store = pltpu.make_async_copy(out_s.at[n, f], out.at[n, f], sem.at[n, f])
            store.start()
            stores.append(store)
    for store in stores:
        store.wait()


VM = pl.BlockSpec(memory_space=pltpu.VMEM)
ANY = pl.BlockSpec(memory_space=pl.ANY)


GRANT = 60
SENT_FIRST = 3
MODE_COST = 20
MIDDLE_COST = 3


def params(mib):
    return pltpu.CompilerParams(vmem_limit_bytes=mib << 20)


def cost(microseconds):
    return pl.CostEstimate(flops=int(microseconds * 1e9), bytes_accessed=0, transcendentals=0)


def shape(*sizes):
    return jax.ShapeDtypeStruct(sizes, F32)


def scratch(*sizes):
    return pltpu.VMEM(sizes, F32)


def like(constant):
    return pltpu.VMEM(constant.shape, constant.dtype)


def per_device(fine_nodes, heating):
    u = fine_nodes.reshape(3, 4, OWN, NX)
    heat = heating.reshape(OWN, NX)
    field = (4, OWN, NX)
    spill = (4, 6 * PLANE, NX)
    near = (4, 2 * PLANE, NX)
    tables = (ALONG, F11, X0, X1, LAM_XY)
    dma = pltpu.SemaphoreType.DMA

    with jax.named_scope("fine"):
        first_c, second_c, to_near, to_across, packet = pl.pallas_call(
            fine_kernel,
            out_shape=[shape(*field), shape(*field), shape(*spill), shape(*spill),
                       shape(SLABS, BLOCKS, 8, 128)],
            in_specs=[ANY] * (2 + len(tables)),
            out_specs=[ANY] * 5,
            scratch_shapes=[scratch(3, 4, OWN, NX), scratch(OWN, NX)] + [like(table) for table in tables] + [
                scratch(*field),
                scratch(4, 12 * PLANE, NX),
                scratch(4, 12 * PLANE, NX),
                scratch(4, 16 * PLANE, NX),
                scratch(4, 16 * PLANE, NX),
                scratch(4, 2, 22 * PLANE, 128),
                scratch(4, 2, 8 * PLANE, 128),
                scratch(4, 4 * CY, CX),
                scratch(4, 18 * CY, CX),
                scratch(4, 16 * CY, CX),
                scratch(SLABS, BLOCKS, 8, 128),
                dma((6,)), dma((3, 4)), dma((4, 6)), dma((4,)),
            ],
            compiler_params=params(GRANT),
        )(u, heat, *tables)

    with jax.named_scope("to_modes"):
        modes = lax.all_to_all(packet.reshape(SLABS * BLOCKS, 8, 128), AXES, 0, 0, tiled=True)

    with jax.named_scope("spill"):
        chip = [(i, i ^ 1) for i in range(BLOCKS)]
        chips = [(i, i + 1) for i in range(1, BLOCKS - 1, 2)]
        from_near = lax.ppermute(to_near, "space", chip)
        from_across = lax.ppermute(to_across, "space", chips + [(j, i) for i, j in chips])

    with jax.named_scope("end"):
        odd = lax.axis_index("space") % 2 == 1
        far = slice(2 * PLANE, 6 * PLANE)

        def ended(fields):
            near, across = from_near[fields, far], from_across[fields, far]
            return second_c[fields] + jnp.concatenate([jnp.where(odd, near, across), jnp.where(odd, across, near)], axis=1)

        most = ended(slice(0, SENT_FIRST))
        rest = ended(slice(SENT_FIRST, 4))

    with jax.named_scope("pass"):
        later = [(i, i + 1) for i in range(SLABS - 1)]
        most_before = lax.ppermute(most, "tm", later)

    with jax.named_scope("modes"):
        constants = (MODE_XY, LAM_Z_COLUMN, LANES, ZF, ZB)
        solved = pl.pallas_call(
            mode_kernel,
            out_shape=shape(SLABS * CZ, 128),
            in_specs=[VM] * 6,
            out_specs=VM,
            cost_estimate=cost(MODE_COST),
            compiler_params=params(16),
        )(modes.reshape(SLABS * BLOCKS * 8, 128), *constants)

    with jax.named_scope("pass_rest"):
        rest_sent, _ = lax.optimization_barrier((rest, solved))
        rest_before = lax.ppermute(rest_sent, "tm", later)

    with jax.named_scope("middle"):
        first, second = pl.pallas_call(
            middle_kernel,
            out_shape=[shape(*field)] * 2,
            in_specs=[ANY] * 6,
            out_specs=[ANY] * 2,
            scratch_shapes=[scratch(*field), scratch(2, *near), scratch(*field), scratch(*field), scratch(2, *field),
                            dma((4, 5)), dma((2, 4))],
            cost_estimate=cost(MIDDLE_COST),
            compiler_params=params(GRANT),
        )(first_c, from_near, from_across, most, rest, u)

    with jax.named_scope("from_modes"):
        solved = solved.reshape(SLABS * BLOCKS, COARSE, 128)
        back = lax.all_to_all(solved, AXES, 0, 0, tiled=True).reshape(SLABS * CZ, 128)

    with jax.named_scope("nodes"):
        out = pl.pallas_call(
            nodes_kernel,
            out_shape=shape(3, *field),
            in_specs=[ANY] * 8,
            out_specs=ANY,
            scratch_shapes=[scratch(SLABS * CZ, 128), scratch(8, 64, 128)] + [scratch(*field)] * 3 + [like(YB), like(XB), scratch(8, OWN // 2, NX), scratch(3, *field), dma((4, 4)), dma((3, 4))],
            cost_estimate=cost(5),
            compiler_params=params(GRANT),
        )(back, first, second, most_before, rest_before, YB, XB, u)
    return out.reshape(1, 3, 4, FINE, NY, NX)


def solution(mesh):
    in_specs = (P("tm", None, None, "space", None, None), P("space", None, None))
    out_specs = P("tm", None, None, "space", None, None)
    return jax.shard_map(
        per_device, mesh=mesh, in_specs=in_specs, out_specs=out_specs, check_vma=False
    )
```

```python
import numpy as np
import jax
import jax.numpy as jnp
from jax import lax
from jax.experimental import pallas as pl
from jax.experimental.pallas import tpu as pltpu
from jax.sharding import PartitionSpec as P

VISCOSITY = 0.4
DIFFUSIVITY = 0.3
SLAB_TIME = 0.25
HALF_TIME = 0.125

SLABS = 8
BLOCKS = 16
NZ, NY, NX = 128, 32, 256
CZ, CY, CX = NZ // 2, NY // 2, NX // 2
FINE = NZ // BLOCKS
COARSE = CZ // BLOCKS
CHUNK = CX // SLABS
SPILL = 5
AXES = ("tm", "space")
F32 = jnp.float32
BF16 = jnp.bfloat16


def real_basis(count):
    j = np.arange(count)
    rows, values = [], []
    for k in range(count):
        theta = 2.0 * np.pi * k / count
        if k == 0:
            row = np.ones(count)
        elif 2 * k == count:
            row = np.cos(np.pi * j)
        elif 2 * k < count:
            row = np.cos(theta * j) * np.sqrt(2.0)
        else:
            row = np.sin(theta * j) * np.sqrt(2.0)
        rows.append(row / np.sqrt(count))
        values.append((32.0 * np.cos(theta) - 2.0 * np.cos(2.0 * theta) - 30.0) / 48.0)
    return np.array(rows), np.array(values)


def pairs(count):
    return np.repeat(np.eye(count), 2, axis=0)


def circulant(count):
    eye = np.eye(count)
    return (
        16.0 * (np.roll(eye, 1, 0) + np.roll(eye, -1, 0))
        - (np.roll(eye, 2, 0) + np.roll(eye, -2, 0))
        - 30.0 * eye
    )


def split(matrix):
    matrix = np.asarray(matrix, np.float32)
    high = matrix.astype(jnp.bfloat16)
    low = (matrix - high.astype(np.float32)).astype(jnp.bfloat16)
    return np.stack([high, low])


FY, LAM_Y = real_basis(CY)
FX, LAM_X = real_basis(CX)


def depth_basis():
    eye = np.eye(CZ)
    band = -30.0 * eye
    for offset, weight in ((1, 16.0), (2, -1.0)):
        band += weight * (np.eye(CZ, k=offset) + np.eye(CZ, k=-offset))
    values, vectors = np.linalg.eigh(band / 48.0)
    return values, vectors


LAM_Z, QZ = depth_basis()

DOWN_X = (FX @ pairs(CX).T * 0.5).T
DOWN_XL = circulant(NX) @ DOWN_X
UP_Y = pairs(CY) @ FY.T
UP_X = FX @ pairs(CX).T


def exact(matrix):
    high = np.asarray(matrix, np.float32).astype(jnp.bfloat16)
    assert np.array_equal(high.astype(np.float64), matrix)
    return high


def stacked(matrix):
    return split(matrix).reshape(-1, matrix.shape[1])


ALONG = exact(circulant(NX))
PLANES = 11
F11 = stacked(np.kron(np.eye(PLANES), FY))
X0 = split(DOWN_X)
X1 = split(DOWN_XL)
LAM_XY = (LAM_Y[:, None] + LAM_X[None, :]).astype(np.float32)


def depth_forward():
    table = np.zeros((2, CZ, BLOCKS, 8))
    for half in range(2):
        for block in range(BLOCKS):
            for slot in range(8):
                z = block * COARSE + half * 8 + slot - SPILL
                if 0 <= z < CZ:
                    table[half, :, block, slot] = QZ[z]
    return table.reshape(2 * CZ, BLOCKS * 8)


ZF = split(depth_forward())
ZB = split(QZ)


def up_y_table():
    table = np.zeros((COARSE, NY, CY, COARSE))
    for z in range(COARSE):
        table[z, :, :, z] = UP_Y
    return table.reshape(COARSE * NY, CY * COARSE)


YB = split(up_y_table())
XB = split(UP_X)


def mode_values():
    table = np.zeros((SLABS, BLOCKS, 2, 4, CHUNK))
    for t in range(SLABS):
        for p in range(BLOCKS):
            table[t, p] = LAM_Y[p] + LAM_X[t * CHUNK:(t + 1) * CHUNK]
    return table.reshape(SLABS * BLOCKS, 128).astype(np.float32)


def lane_constants():
    own = np.array([VISCOSITY, VISCOSITY, VISCOSITY, DIFFUSIVITY])
    partner = np.array([VISCOSITY, VISCOSITY, DIFFUSIVITY, VISCOSITY])
    couple = np.array([2.0, -2.0, 1.0, 1.0])
    product = np.array([-4.0, -4.0, 1.0, 1.0])
    table = np.zeros((8, 2, 4, CHUNK))
    for row, values in enumerate((own, partner, couple, product)):
        table[row] = values[None, :, None]
    return table.reshape(8, 128).astype(np.float32)


MODE_XY = mode_values()
LANES = lane_constants()
LAM_Z_COLUMN = np.repeat(LAM_Z[:, None], 128, axis=1).astype(np.float32)


def halves(x):
    high = x.astype(BF16)
    return high, (x - high.astype(F32)).astype(BF16)


def dot(a, b):
    return jnp.dot(a, b, preferred_element_type=F32)


def left(table, x):
    high, low = halves(x)
    return dot(table[0], high) + (dot(table[0], low) + dot(table[1], high))


def right(x, table):
    high, low = halves(x)
    return dot(high, table[0]) + (dot(low, table[0]) + dot(high, table[1]))


def rolled(x, by, axis):
    return pltpu.roll(x, by % x.shape[axis], axis)


def across_y(x):
    near = rolled(x, 1, 0) + rolled(x, -1, 0)
    far = rolled(x, 2, 0) + rolled(x, -2, 0)
    return 16.0 * near - far


def total(terms):
    out = terms[0]
    for term in terms[1:]:
        out = out + term
    return out


def chunk_transpose(values):
    values = list(values)
    lane = lax.broadcasted_iota(jnp.int32, values[0].shape, 1)
    for bit in (1, 2, 4):
        shift = CHUNK * bit
        low = (lane & shift) == 0
        for i in range(8):
            if i & bit:
                continue
            j = i | bit
            first, second = values[i], values[j]
            values[i] = jnp.where(low, first, rolled(second, shift, 1))
            values[j] = jnp.where(low, rolled(first, -shift, 1), second)
    return values


def left_stacked(table, x):
    high, low = halves(x)
    rows = table.shape[0] // 2
    both = dot(table, high)
    return both[:rows] + (both[rows:] + dot(table[:rows], low))


PLANE = NY
OWN = FINE * PLANE


def position():
    tm, space = lax.axis_index("tm"), lax.axis_index("space")
    one = jnp.float32(1.0)
    zero = jnp.float32(0.0)
    return jnp.where(tm > 0, one, zero), jnp.where(space > 0, one, zero), jnp.where(space < BLOCKS - 1, one, zero)


def fine_kernel(u_hbm, q_hbm, along_hbm, f11_hbm, x0_hbm, x1_hbm, lam_hbm,
                first_hbm, second_hbm, near_hbm, across_hbm, send_hbm,
                u, q, along, f11, x0, x1, lam,
                a_s, fe, be, se, cs, rows_s, pair_s, y_s, w_s, g_s, send_s, in_sem, u_sem, out_sem, send_sem):
    mu, keep_low, keep_high = position()
    loads = [
        pltpu.make_async_copy(source, target, in_sem.at[i])
        for i, (source, target) in enumerate((
            (along_hbm, along), (x0_hbm, x0), (x1_hbm, x1), (f11_hbm, f11), (lam_hbm, lam), (q_hbm, q)))
    ]
    node_loads = [
        [pltpu.make_async_copy(u_hbm.at[n, f], u.at[n, f], u_sem.at[n, f]) for n in range(3)] for f in range(4)
    ]
    for load in node_loads[0] + loads[:1] + node_loads[1] + loads[1:5] + node_loads[2] + node_loads[3] + loads[5:]:
        load.start()

    edge = 2 * PLANE
    middle = pl.ds(edge, OWN)
    odd = lax.axis_index("space") % 2
    sides = ((near_hbm, 1 - odd), (across_hbm, odd))
    stores = []

    def store(source, target, sem):
        copy = pltpu.make_async_copy(source, target, sem)
        copy.start()
        stores.append(copy)

    def field(f):
        nu = DIFFUSIVITY if f == 3 else VISCOSITY
        return nu, (2.0, -2.0, 1.0, 1.0)[f], f ^ 1

    def fine_plane(ref, f, p, low):
        return ref[f, pl.ds((p - low) * PLANE, PLANE)]

    def depth(ref, f, p, low, high):
        near = [fine_plane(ref, f, p + o, low) for o in (-1, 1) if low <= p + o < high]
        far = [fine_plane(ref, f, p + o, low) for o in (-2, 2) if low <= p + o < high]
        if not near:
            return -total(far)
        return 16.0 * total(near) - total(far) if far else 16.0 * total(near)

    def along_x(x):
        high, low = halves(x)
        return dot(high, along[...]) + dot(low, along[...])

    def combine(f):
        for load in node_loads[f]:
            load.wait()
        a_s[f] = (5.0 / 24.0) * u[0, f] + (1.0 / 3.0) * u[1, f] - (1.0 / 24.0) * u[2, f]

    def first_stage(f):
        nu, couple, partner = field(f)
        scale = nu * (SLAB_TIME / 12.0)
        row = along_x(a_s[f])
        for p in range(-2, FINE + 2):
            here = pl.ds((p + 2) * PLANE, PLANE)
            acc = depth(a_s, f, p, 0, FINE)
            if 0 <= p < FINE:
                own = pl.ds(p * PLANE, PLANE)
                centre = a_s[f, own]
                start = u[0, f, own]
                acc = acc + (across_y(centre) - 60.0 * centre) + row[p * PLANE:(p + 1) * PLANE]
                value = scale * acc + (couple * SLAB_TIME) * a_s[partner, own] + start
                if f == 3:
                    value = value + HALF_TIME * q[own]
                be[f, here] = 0.5 * value + ((-1.0 / 24.0) * start - (1.0 / 6.0) * u[1, f, own] + (5.0 / 24.0) * u[2, f, own])
            else:
                value = (scale * (keep_low if p < 0 else keep_high)) * acc
                be[f, here] = 0.5 * value
            fe[f, here] = value
        store(fe.at[f, middle], first_hbm.at[f], out_sem.at[f, 0])
        for i, (target, up) in enumerate(sides):
            rows = pl.ds(pl.multiple_of(up * (edge + OWN), edge), edge)
            store(fe.at[f, rows], target.at[f, pl.ds(0, edge)], out_sem.at[f, 1 + i])

    def second_stage(f):
        nu, couple, partner = field(f)
        scale = nu * (SLAB_TIME / 12.0)
        row = along_x(be[f])
        for p in range(-4, FINE + 4):
            here = pl.ds((p + 4) * PLANE, PLANE)
            acc = depth(be, f, p, -2, FINE + 2)
            mask = keep_low if p < 0 else keep_high
            if -2 <= p < FINE + 2:
                inner = pl.ds((p + 2) * PLANE, PLANE)
                centre = be[f, inner]
                first = fe[f, inner]
                acc = acc + (across_y(centre) - 60.0 * centre) + row[(p + 2) * PLANE:(p + 3) * PLANE]
                value = scale * acc + (couple * SLAB_TIME) * be[partner, inner] + first
                if 0 <= p < FINE:
                    own = pl.ds(p * PLANE, PLANE)
                    if f == 3:
                        value = value + HALF_TIME * q[own]
                    c = (1.0 / 6.0) * (value + u[0, f, own]) + (2.0 / 3.0) * first
                else:
                    value = mask * value
                    c = (1.0 / 6.0) * value + (2.0 / 3.0) * first
            else:
                value = (scale * mask) * acc
                c = (1.0 / 6.0) * value
            se[f, here] = value
            cs[f, here] = c
        store(se.at[f, pl.ds(2 * edge, OWN)], second_hbm.at[f], out_sem.at[f, 3])
        for i, (target, up) in enumerate(sides):
            rows = pl.ds(pl.multiple_of(up * (2 * edge + OWN), edge), 2 * edge)
            store(se.at[f, rows], target.at[f, pl.ds(edge, 2 * edge)], out_sem.at[f, 4 + i])

    def put(ref, f, k, value):
        for i in range(2):
            ref[f, i, pl.ds(k * PLANE, PLANE)] = value[:, i * 128:(i + 1) * 128]

    def every_other(ref, f, start, count):
        return jnp.concatenate([ref[f, i, pl.ds(start, count, stride=2), :] for i in range(2)], axis=1)

    def coarse_means(f):
        nu, couple, partner = field(f)
        scale = nu * (SLAB_TIME / 12.0)

        def pair_sum(ref, g, k):
            return fine_plane(ref, g, 2 * k, -4) + fine_plane(ref, g, 2 * k + 1, -4)

        for k in range(-3, COARSE + 3):
            value = None
            inside = -2 <= k < COARSE + 2
            if inside:
                mean = pair_sum(cs, f, k)
                put(pair_s, f, k + 2, mean)
                value = (-7.0 * scale) * mean + (couple * (SLAB_TIME * 0.5)) * pair_sum(cs, partner, k)
            for weight, planes in ((7.5, (2 * k - 1, 2 * k + 2)), (-0.5, (2 * k - 2, 2 * k + 3))):
                part = [fine_plane(cs, f, p, -4) for p in planes if -4 <= p < FINE + 4]
                if part:
                    part = (weight * scale) * total(part)
                    value = part if value is None else value + part
            if f == 3 and 0 <= k < COARSE:
                value = value + (0.5 * SLAB_TIME) * (q[pl.ds(2 * k * PLANE, PLANE)] + q[pl.ds((2 * k + 1) * PLANE, PLANE)])
            if k < 0:
                value = keep_low * value
            if k >= COARSE:
                value = keep_high * value
            if inside:
                last = 0.5 * pair_sum(se, f, k)
                value = value - last
                if 0 <= k < COARSE:
                    start = 0.5 * (u[0, f, pl.ds(2 * k * PLANE, PLANE)] + u[0, f, pl.ds((2 * k + 1) * PLANE, PLANE)])
                    value = value + start
                    last = last - mu * start
                    put(rows_s, f, 18 + k, start)
                put(rows_s, f, 12 + k, last)
            put(rows_s, f, k + 3, value)

    def across(f):
        nu, _, _ = field(f)
        scale = nu * (SLAB_TIME / 12.0)
        count = 22 * CY
        y = 0.5 * (every_other(rows_s, f, 0, count) + every_other(rows_s, f, 1, count))
        even = every_other(pair_s, f, 0, 8 * CY)
        odd = every_other(pair_s, f, 1, 8 * CY)
        mean = even + odd
        curved = []
        for k in range(8):
            rows = slice(k * CY, (k + 1) * CY)
            e, o = even[rows], odd[rows]
            near = rolled(o, 1, 0) + rolled(e, -1, 0)
            far = rolled(e, 1, 0) + rolled(o, -1, 0)
            value = (0.25 * scale) * (15.0 * near - far - 14.0 * mean[rows])
            if k < 2:
                value = keep_low * value
            if k >= 6:
                value = keep_high * value
            curved.append(value)
        y = jnp.concatenate([y[:CY], y[CY:9 * CY] + jnp.concatenate(curved, axis=0), y[9 * CY:]], axis=0)
        both = right(y, x0)
        bent = (0.25 * scale) * right(mean, x1)
        return jnp.concatenate([both[:CY], both[CY:9 * CY] + bent, both[9 * CY:]], axis=0)

    def to_y_modes(pair):
        both = jnp.concatenate([across(f) for f in pair], axis=1)
        half = PLANES * CY
        out = [left_stacked(f11[...], both[i * half:(i + 1) * half]) for i in range(2)]
        out = jnp.concatenate(out, axis=0)
        for i, f in enumerate(pair):
            lanes = slice(i * CX, (i + 1) * CX)
            w_s[f] = out[:18 * CY, lanes]
            y_s[f] = out[18 * CY:, lanes]

    def kept(value, p, count):
        if p < 0:
            return value * keep_low
        if p >= count:
            return value * keep_high
        return value

    def plane(ref, f, k, low, high):
        if low <= k < high:
            return ref[f, pl.ds((k - low) * CY, CY)]
        return None

    def node_plane(f, k):
        if -2 <= k < COARSE + 2:
            return w_s[f, pl.ds((12 + k) * CY, CY)]
        return None

    def coarse_slope(ref, f, k, low, high):
        nu, couple, partner = field(f)
        out = None
        for weight, offsets in ((16.0 / 48.0, (-1, 1)), (-1.0 / 48.0, (-2, 2))):
            part = [plane(ref, f, k + o, low, high) for o in offsets]
            part = [value for value in part if value is not None]
            if part:
                part = weight * total(part)
                out = part if out is None else out + part
        centre = plane(ref, f, k, low, high)
        if centre is None:
            return nu * out
        out = out + (lam[...] - 30.0 / 48.0) * centre
        return nu * out + couple * plane(ref, partner, k, low, high)

    def defect(f):
        for k in range(-2, COARSE + 2):
            value = coarse_slope(y_s, f, k, 0, COARSE)
            value = kept((mu * SLAB_TIME) * value, k, COARSE)
            rows = pl.ds((k + 3) * CY, CY)
            w_s[f, rows] = w_s[f, rows] - value

    def packet(f):
        for k in range(-SPILL, 16 - SPILL):
            rows = pl.ds((k + SPILL) * CY, CY)
            if k >= COARSE + SPILL:
                g_s[f, rows] = jnp.zeros((CY, CX), F32)
                continue
            value = kept(HALF_TIME * coarse_slope(w_s, f, k, -3, COARSE + 3), k, COARSE)
            for part in (plane(w_s, f, k, -3, COARSE + 3), node_plane(f, k)):
                if part is not None:
                    value = value + part
            g_s[f, rows] = value

    for pair in ((0, 1), (2, 3)):
        for f in pair:
            combine(f)
        if pair[0] == 0:
            loads[0].wait()
        else:
            loads[5].wait()
        for f in pair:
            first_stage(f)
        for f in pair:
            second_stage(f)
        for f in pair:
            coarse_means(f)
        if pair[0] == 0:
            for load in loads[1:5]:
                load.wait()
        to_y_modes(pair)
        for stage in (defect, packet):
            for f in pair:
                stage(f)

    def pack(p):
        values = []
        for half in range(2):
            for f in range(4):
                values.append(g_s[f, pl.ds(half * 8 * CY + p, 8, stride=CY), :])
        for t, value in enumerate(chunk_transpose(values)):
            send_s[t, p] = value

    step = BLOCKS // 4
    for i in range(4):
        for p in range(i * step, (i + 1) * step):
            pack(p)
        part = pl.ds(i * step, step)
        store(send_s.at[:, part], send_hbm.at[:, part], send_sem.at[i])
    for copy in stores:
        copy.wait()


def mode_kernel(g, xy, lam_z, lanes, zf, zb, out):
    index = lax.axis_index("tm") * BLOCKS + lax.axis_index("space")
    lam = lam_z[...] + xy[pl.ds(index, 1)]
    nu, other, couple, product = (lanes[pl.ds(i, 1)] for i in range(4))
    own = nu * lam
    partner = other * lam
    half_square = 0.5 * SLAB_TIME * SLAB_TIME
    diagonal = 1.0 + SLAB_TIME * own + half_square * (own * own + product)
    mixing = couple * (SLAB_TIME + half_square * (own + partner))
    lane = lax.broadcasted_iota(jnp.int32, (CZ, 128), 1)
    even = (lane & CHUNK) == 0
    left_half = lane < 64

    state = None
    states = [jnp.zeros((CZ, 128), F32)]
    for s in range(SLABS):
        both = left(zf, g[pl.ds(s * BLOCKS * 8, BLOCKS * 8)])
        source = both[:CZ] + rolled(both[CZ:], 64, 1)
        if state is None:
            state = source
        else:
            swapped = jnp.where(even, rolled(state, -CHUNK, 1), rolled(state, CHUNK, 1))
            state = diagonal * state + mixing * swapped + source
        state = jnp.where(left_half, state, 0.0)
        states.append(state)
    for s in range(SLABS):
        packed = states[s] + rolled(states[s + 1], 64, 1)
        out[pl.ds(s * CZ, CZ)] = left(zb, packed)


def paired(x, axis):
    index = lax.broadcasted_iota(jnp.int32, x.shape, axis)
    return x + jnp.where((index & 1) == 0, rolled(x, -1, axis), rolled(x, 1, axis))


def block_mean(x, weight):
    return paired(paired(weight * x, 0), 1)


def middle_kernel(first_hbm, near_hbm, across_hbm, most_hbm, rest_hbm, u_hbm, first_out, second_out,
                  first, spill, second, u, out, in_sem, out_sem):
    mu, _, _ = position()
    odd = lax.axis_index("space") % 2
    part = pl.ds(0, 2 * PLANE)
    loads = []
    for f in range(4):
        source = most_hbm.at[f] if f < SENT_FIRST else rest_hbm.at[f - SENT_FIRST]
        moves = ((first_hbm.at[f], first.at[f]), (near_hbm.at[f, part], spill.at[0, f]), (across_hbm.at[f, part], spill.at[1, f]),
                 (source, second.at[f]), (u_hbm.at[0, f], u.at[f]))
        for i, (source, target) in enumerate(moves):
            load = pltpu.make_async_copy(source, target, in_sem.at[f, i])
            load.start()
            loads.append(load)
    stores = []
    for f in range(4):
        for load in loads[5 * f:5 * f + 5]:
            load.wait()
        for k in range(COARSE):
            pair = [pl.ds((2 * k + i) * PLANE, PLANE) for i in range(2)]
            seconds = [second[f, rows] for rows in pair]
            mean = block_mean(seconds[0] + seconds[1], 0.125)
            start = block_mean(u[f, pair[0]] + u[f, pair[1]], 0.125 * mu)
            middle = 0.5 * (mean + start)
            for i, rows in enumerate(pair):
                p = 2 * k + i
                value = first[f, rows] - middle
                if p < 2:
                    value = value + spill[1 - odd, f, pl.ds(p * PLANE, PLANE)]
                if p >= FINE - 2:
                    value = value + spill[odd, f, pl.ds((p - FINE + 2) * PLANE, PLANE)]
                out[0, f, rows] = value
                out[1, f, rows] = seconds[i] - mean
        for n, target in enumerate((first_out, second_out)):
            store = pltpu.make_async_copy(out.at[n, f], target.at[f], out_sem.at[n, f])
            store.start()
            stores.append(store)
    for store in stores:
        store.wait()


def doubled(x):
    return jnp.concatenate([x[(p // 2) * PLANE:(p // 2 + 1) * PLANE] for p in range(FINE)], axis=0)


def nodes_kernel(modes_hbm, first_hbm, second_hbm, most_hbm, rest_hbm, yb_hbm, xb_hbm, u_hbm, out, modes, h_s, first, second, before, yb, xb, p_s, out_s, in_sem, sem):
    mu, _, _ = position()
    leading = lax.axis_index("tm") == 0
    arrived = pltpu.make_async_copy(modes_hbm, modes, in_sem.at[2, 3])
    tables = [pltpu.make_async_copy(yb_hbm, yb, in_sem.at[0, 3]), pltpu.make_async_copy(xb_hbm, xb, in_sem.at[1, 3])]
    for load in [arrived] + tables:
        load.start()
    for f in range(4):
        for i, (source, target) in enumerate(((first_hbm, first), (second_hbm, second))):
            pltpu.make_async_copy(source.at[f], target.at[f], in_sem.at[f, i]).start()

        @pl.when(leading)
        def _():
            pltpu.make_async_copy(u_hbm.at[0, f], before.at[f], in_sem.at[f, 2]).start()

        @pl.when(jnp.logical_not(leading))
        def _():
            source = most_hbm.at[f] if f < SENT_FIRST else rest_hbm.at[f - SENT_FIRST]
            pltpu.make_async_copy(source, before.at[f], in_sem.at[f, 2]).start()

    arrived.wait()
    for r in range(8):
        values = [modes[pl.ds(t * 64 + r * 8, 8)] for t in range(SLABS)]
        for g, value in enumerate(chunk_transpose(values)):
            h_s[g, pl.ds(r * 8, 8)] = value
    for load in tables:
        load.wait()
    for g in range(8):
        p_s[g] = right(left(yb, h_s[g]), xb)
    stores = []

    def send(n, f):
        store = pltpu.make_async_copy(out_s.at[n, f], out.at[n, f], sem.at[n, f])
        store.start()
        stores.append(store)

    for f in range(4):
        start = p_s[f]
        end = p_s[4 + f]
        pltpu.make_async_copy(first_hbm.at[f], first.at[f], in_sem.at[f, 0]).wait()
        out_s[1, f] = first[f] + doubled(0.5 * (start + end))
        send(1, f)
        pltpu.make_async_copy(second_hbm.at[f], second.at[f], in_sem.at[f, 1]).wait()
        out_s[2, f] = second[f] + doubled(end)
        send(2, f)
        pltpu.make_async_copy(second_hbm.at[f], before.at[f], in_sem.at[f, 2]).wait()
        for k in range(COARSE):
            pair = [pl.ds((2 * k + i) * PLANE, PLANE) for i in range(2)]
            value = [before[f, rows] for rows in pair]
            shift = start[k * PLANE:(k + 1) * PLANE] - block_mean(value[0] + value[1], 0.125 * mu)
            for i, rows in enumerate(pair):
                out_s[0, f, rows] = value[i] + shift
        send(0, f)
    for store in stores:
        store.wait()


VM = pl.BlockSpec(memory_space=pltpu.VMEM)
ANY = pl.BlockSpec(memory_space=pl.ANY)


GRANT = 60
SENT_FIRST = 3
MODE_COST = 20
MIDDLE_COST = 3


def params(mib):
    return pltpu.CompilerParams(vmem_limit_bytes=mib << 20)


def cost(microseconds):
    return pl.CostEstimate(flops=int(microseconds * 1e9), bytes_accessed=0, transcendentals=0)


def shape(*sizes):
    return jax.ShapeDtypeStruct(sizes, F32)


def scratch(*sizes):
    return pltpu.VMEM(sizes, F32)


def like(constant):
    return pltpu.VMEM(constant.shape, constant.dtype)


def per_device(fine_nodes, heating):
    u = fine_nodes.reshape(3, 4, OWN, NX)
    heat = heating.reshape(OWN, NX)
    field = (4, OWN, NX)
    spill = (4, 6 * PLANE, NX)
    near = (4, 2 * PLANE, NX)
    tables = (ALONG, F11, X0, X1, LAM_XY)
    dma = pltpu.SemaphoreType.DMA

    with jax.named_scope("fine"):
        first_c, second_c, to_near, to_across, packet = pl.pallas_call(
            fine_kernel,
            out_shape=[shape(*field), shape(*field), shape(*spill), shape(*spill),
                       shape(SLABS, BLOCKS, 8, 128)],
            in_specs=[ANY] * (2 + len(tables)),
            out_specs=[ANY] * 5,
            scratch_shapes=[scratch(3, 4, OWN, NX), scratch(OWN, NX)] + [like(table) for table in tables] + [
                scratch(*field),
                scratch(4, 12 * PLANE, NX),
                scratch(4, 12 * PLANE, NX),
                scratch(4, 16 * PLANE, NX),
                scratch(4, 16 * PLANE, NX),
                scratch(4, 2, 22 * PLANE, 128),
                scratch(4, 2, 8 * PLANE, 128),
                scratch(4, 4 * CY, CX),
                scratch(4, 18 * CY, CX),
                scratch(4, 16 * CY, CX),
                scratch(SLABS, BLOCKS, 8, 128),
                dma((6,)), dma((3, 4)), dma((4, 6)), dma((4,)),
            ],
            compiler_params=params(GRANT),
        )(u, heat, *tables)

    with jax.named_scope("to_modes"):
        modes = lax.all_to_all(packet.reshape(SLABS * BLOCKS, 8, 128), AXES, 0, 0, tiled=True)

    with jax.named_scope("spill"):
        chip = [(i, i ^ 1) for i in range(BLOCKS)]
        chips = [(i, i + 1) for i in range(1, BLOCKS - 1, 2)]
        from_near = lax.ppermute(to_near, "space", chip)
        from_across = lax.ppermute(to_across, "space", chips + [(j, i) for i, j in chips])

    with jax.named_scope("end"):
        odd = lax.axis_index("space") % 2 == 1
        far = slice(2 * PLANE, 6 * PLANE)

        def ended(fields):
            near, across = from_near[fields, far], from_across[fields, far]
            return second_c[fields] + jnp.concatenate([jnp.where(odd, near, across), jnp.where(odd, across, near)], axis=1)

        most = ended(slice(0, SENT_FIRST))
        rest = ended(slice(SENT_FIRST, 4))

    with jax.named_scope("pass"):
        later = [(i, i + 1) for i in range(SLABS - 1)]
        most_before = lax.ppermute(most, "tm", later)

    with jax.named_scope("modes"):
        constants = (MODE_XY, LAM_Z_COLUMN, LANES, ZF, ZB)
        solved = pl.pallas_call(
            mode_kernel,
            out_shape=shape(SLABS * CZ, 128),
            in_specs=[VM] * 6,
            out_specs=VM,
            cost_estimate=cost(MODE_COST),
            compiler_params=params(16),
        )(modes.reshape(SLABS * BLOCKS * 8, 128), *constants)

    with jax.named_scope("pass_rest"):
        rest_sent, _ = lax.optimization_barrier((rest, solved))
        rest_before = lax.ppermute(rest_sent, "tm", later)

    with jax.named_scope("middle"):
        first, second = pl.pallas_call(
            middle_kernel,
            out_shape=[shape(*field)] * 2,
            in_specs=[ANY] * 6,
            out_specs=[ANY] * 2,
            scratch_shapes=[scratch(*field), scratch(2, *near), scratch(*field), scratch(*field), scratch(2, *field),
                            dma((4, 5)), dma((2, 4))],
            cost_estimate=cost(MIDDLE_COST),
            compiler_params=params(GRANT),
        )(first_c, from_near, from_across, most, rest, u)

    with jax.named_scope("from_modes"):
        solved = solved.reshape(SLABS * BLOCKS, COARSE, 128)
        back = lax.all_to_all(solved, AXES, 0, 0, tiled=True).reshape(SLABS * CZ, 128)

    with jax.named_scope("nodes"):
        out = pl.pallas_call(
            nodes_kernel,
            out_shape=shape(3, *field),
            in_specs=[ANY] * 8,
            out_specs=ANY,
            scratch_shapes=[scratch(SLABS * CZ, 128), scratch(8, 64, 128)] + [scratch(*field)] * 3 + [like(YB), like(XB), scratch(8, OWN // 2, NX), scratch(3, *field), dma((4, 4)), dma((3, 4))],
            cost_estimate=cost(5),
            compiler_params=params(GRANT),
        )(back, first, second, most_before, rest_before, YB, XB, u)
    return out.reshape(1, 3, 4, FINE, NY, NX)


def solution(mesh):
    in_specs = (P("tm", None, None, "space", None, None), P("space", None, None))
    out_specs = P("tm", None, None, "space", None, None)
    return jax.shard_map(
        per_device, mesh=mesh, in_specs=in_specs, out_specs=out_specs, check_vma=False
    )
```
